256 devices in a mesh: seq: 32 (over y, z), head: 2 (over core), pool: 4 (over x).
Axes of the slice: x: 4, y: 4, z: 8, core: 2. Of those that a mesh axis runs over, the one named last changes fastest.
Arguments:
- prefill_hidden: bfloat16 [4096, 7168], P('seq', ('head', 'pool')), may hold values from -6 to 6
- down_weight: bfloat16 [7168, 576], P(('head', 'pool')), may hold values from -0.0625 to 0.0625
- latent_gain: float32 [512], replicated, may hold values from 0.1 to 1.9
- key_weight: bfloat16 [512, 16384], P(None, ('head', 'pool')), may hold values from -0.25 to 0.25
- value_weight: bfloat16 [512, 16384], P(None, ('head', 'pool')), may hold values from -0.25 to 0.25
- prefill_query: bfloat16 [4096, 24576], P('seq', ('head', 'pool')), may hold values from -240 to 240
- decode_hidden: bfloat16 [2, 128, 7168], P(None, 'seq', ('head', 'pool')), may hold values from -6 to 6
- decode_query: bfloat16 [2, 128, 24576], P(None, 'seq', ('head', 'pool')), may hold values from -240 to 240
- latent_cache: bfloat16 [128, 512, 576], P('seq'), may hold values from -6 to 6
- place_device: int32 [4096], P('seq'), may hold values from 0 to 31, as said below
- place_slot: int32 [4096], P('seq'), may hold values from 0 to 2047, as said below
- context_length: int32 [128], P('seq'), may hold values from 1 to 512, as said below
Outputs:
- prefill_out: bfloat16 [4096, 16384], P('seq', ('head', 'pool'))
- decode_out: bfloat16 [2, 128, 16384], P(None, 'seq', ('head', 'pool'))
The draws below stay inside these ranges and needn't reach their ends.
Inputs may be any that keep to these rules, and one draw needn't show every extreme that they name: `place_device`: each block of 128 consecutive tokens sends at most 8 tokens to one decode index, and exactly 8 to one of them. With place_device every token names its own slot; the position place_slot % 512 is below context_length of the row it names. `context_length`: some row has exactly 512.
All inputs are finite; a program needn't handle non-finite values.
Results may differ from the reference program's by a relative error of at most 0.012.
The reference program's roundings to bfloat16 on the way count: a program that leaves them out, or rounds other values in their place, can miss the bound.
Values may be sent and summed in bfloat16 or wider, within the bound.
A program may use at most 64 MiB of HBM per device.

```python
import jax
import jax.numpy as jnp
from jax import lax

D = 7168
H = 128
LAT = 512
ROPE = 64
NOPE = 128
VDIM = 128
TOK_DEV = 128
PROMPTS = 1
ROWS_DEV = 4
STEPS = 2
CTX = 512
TOKENS = 4096
ROWS = 128
CAP = 8
N_SEQ = 32


def placement(key):
    hot_key, order_key, offset_key, older_key, chosen_key = jax.random.split(key, 5)
    hottest = jax.random.randint(hot_key, (N_SEQ,), 0, N_SEQ, dtype=jnp.int32)
    ranks = jax.vmap(lambda single: jax.random.permutation(single, TOK_DEV))(jax.random.split(order_key, N_SEQ)).astype(jnp.int32)
    offset = jax.random.randint(offset_key, (N_SEQ,), 0, N_SEQ - 1, dtype=jnp.int32)
    spread = (hottest[:, None] + 1 + (offset[:, None] + ranks - CAP) % (N_SEQ - 1)) % N_SEQ
    device = jnp.where(ranks < CAP, hottest[:, None], spread).reshape(TOKENS).astype(jnp.int32)
    marks = (device[:, None] == jnp.arange(N_SEQ, dtype=jnp.int32)[None, :]).astype(jnp.int32)
    arrival = jnp.sum((jnp.cumsum(marks, 0) - marks) * marks, 1)
    count = jnp.sum(marks, 0)
    local_row = arrival % ROWS_DEV
    depth = arrival // ROWS_DEV
    incoming = ((count[:, None] - jnp.arange(ROWS_DEV, dtype=jnp.int32)[None, :] + ROWS_DEV - 1) // ROWS_DEV).reshape(ROWS)
    older = jax.random.randint(older_key, (ROWS,), 1, CTX - incoming + 1, dtype=jnp.int32)
    chosen = jax.random.randint(chosen_key, (), 0, ROWS, dtype=jnp.int32)
    older = jnp.where(jnp.arange(ROWS, dtype=jnp.int32) == chosen, CTX - incoming, older)
    slot = local_row * CTX + older[device * ROWS_DEV + local_row] + depth
    return (device, slot.astype(jnp.int32), (older + incoming).astype(jnp.int32))


def draw_place_device(key, part):
    return placement(key)[0]


def draw_place_slot(key, part):
    return placement(key)[1]


def draw_context_length(key, part):
    return placement(key)[2]


def draw_prefill_query(key, part):
    key = jax.random.fold_in(key, 11)
    return (3.0 * jax.random.truncated_normal(key, -6.0, 6.0, (TOKENS, H * (NOPE + ROPE)))).astype(jnp.bfloat16)


def draw_decode_query(key, part):
    key = jax.random.fold_in(key, 23)
    return (3.0 * jax.random.truncated_normal(key, -6.0, 6.0, (STEPS, ROWS, H * (NOPE + ROPE)))).astype(jnp.bfloat16)


def level_of(own_key, shape, pieces, least, largest):
    factor_of = 1.0
    for axis_at, blocks in pieces:
        draws = jax.random.uniform(jax.random.fold_in(jax.random.fold_in(own_key, 6), axis_at), (blocks,), jnp.float32, least / len(pieces), largest / len(pieces))
        factor_of = factor_of * jnp.repeat(jnp.exp(draws), shape[axis_at] // blocks).reshape((-1,) + (1,) * (len(shape) - 1 - axis_at))
    return factor_of


def gaussian(stream_key, extent, scale, bound, cuts=(), kind=jnp.bfloat16):
    array = scale * jax.random.normal(stream_key, extent, jnp.float32)
    if cuts:
        array = array * level_of(stream_key, extent, cuts, -0.22, 0.18)
    return jnp.clip(array, -bound, bound).astype(kind)


def setup_inputs(seed: int = 0) -> dict:
    key_of = jax.random.split(jax.random.key(seed), 13)
    prefill_hidden = gaussian(key_of[0], (TOKENS, D), 1.0, 6.0, ((0, 32), (1, 8)))
    down_weight = gaussian(key_of[1], (D, LAT + ROPE), D ** -0.5, 0.0625, ((0, 8),))
    latent_gain = jnp.clip(1.0 + 0.18 * jax.random.normal(key_of[2], (LAT,), jnp.float32), 0.1, 1.9)
    key_weight = gaussian(key_of[3], (LAT, H * NOPE), LAT ** -0.5, 0.25, ((1, 8),))
    value_weight = gaussian(key_of[4], (LAT, H * VDIM), LAT ** -0.5, 0.25, ((1, 8),))
    prefill_query = draw_prefill_query(jax.random.fold_in(key_of[12], 71), 0)
    decode_hidden = gaussian(key_of[6], (STEPS, ROWS, D), 1.0, 6.0, ((1, 32), (2, 8)))
    decode_query = draw_decode_query(jax.random.fold_in(key_of[12], 71), 0)
    latent_cache = gaussian(key_of[8], (ROWS, CTX, LAT + ROPE), 1.0, 6.0, ((0, 32),))
    place_device = draw_place_device(jax.random.fold_in(key_of[12], 71), 0)
    place_slot = draw_place_slot(jax.random.fold_in(key_of[12], 71), 0)
    context_length = draw_context_length(jax.random.fold_in(key_of[12], 71), 0)
    return dict(prefill_hidden=prefill_hidden, down_weight=down_weight, latent_gain=latent_gain, key_weight=key_weight, value_weight=value_weight, prefill_query=prefill_query, decode_hidden=decode_hidden, decode_query=decode_query, latent_cache=latent_cache, place_device=place_device, place_slot=place_slot, context_length=context_length)


def rounded(values):
    return lax.optimization_barrier(values.astype(jnp.bfloat16)).astype(jnp.float32)

def rotate(part, position):
    half = part.shape[-1] // 2
    freq = 10000.0 ** (-jnp.arange(half, dtype=jnp.float32) / half)
    angle = position[..., None] * freq
    first_half = part[..., :half]
    second_half = part[..., half:]
    cosine = jnp.cos(angle)
    sine = jnp.sin(angle)
    return jnp.concatenate([first_half * cosine - second_half * sine, second_half * cosine + first_half * sine], -1)

def finalize(summed, latent_gain, position):
    content = summed[..., :LAT]
    meansq = lax.optimization_barrier(jnp.mean(content * content, -1, keepdims=True))
    content = content * lax.rsqrt(meansq + 1e-06) * latent_gain.astype(jnp.float32)
    return jnp.concatenate([content, rotate(summed[..., LAT:], position)], -1).astype(jnp.bfloat16)

def reference(prefill_hidden, down_weight, latent_gain, key_weight, value_weight, prefill_query, decode_hidden, decode_query, latent_cache, place_device, place_slot, context_length):
    factor = (NOPE + ROPE) ** (-0.5)
    prompt_len = TOKENS // PROMPTS
    summed = jnp.dot(prefill_hidden, down_weight, preferred_element_type=jnp.float32)
    position = (jnp.arange(TOKENS, dtype=jnp.int32) % prompt_len).astype(jnp.float32)
    latent = finalize(summed, latent_gain, position)
    grouped = latent.reshape(PROMPTS, prompt_len, LAT + ROPE).astype(jnp.float32)
    query = prefill_query.reshape(PROMPTS, prompt_len, H, NOPE + ROPE).transpose(2, 0, 1, 3)
    key_heads = key_weight.reshape(LAT, H, NOPE).transpose(1, 0, 2)
    value_heads = value_weight.reshape(LAT, H, VDIM).transpose(1, 0, 2)
    causal = jnp.tril(jnp.ones((prompt_len, prompt_len), dtype=bool))

    def one_head(items):
        head_query, head_key, head_value = items
        knope = rounded(jnp.einsum('pkc,cd->pkd', grouped[..., :LAT], head_key.astype(jnp.float32)))
        values = rounded(jnp.einsum('pkc,cd->pkd', grouped[..., :LAT], head_value.astype(jnp.float32)))
        head_query = head_query.astype(jnp.float32)
        scores = jnp.einsum('pqd,pkd->pqk', head_query[..., :NOPE], knope)
        scores = scores + jnp.einsum('pqd,pkd->pqk', head_query[..., NOPE:], grouped[..., LAT:])
        scores = jnp.where(causal, scores * factor, -1e+30)
        peak = lax.optimization_barrier(jnp.max(scores, -1, keepdims=True))
        expo = jnp.where(causal, jnp.exp(scores - peak), 0.0)
        total = lax.optimization_barrier(jnp.sum(expo, -1, keepdims=True))
        mixed = jnp.einsum('pqk,pkd->pqd', rounded(expo), values) / total
        return mixed.astype(jnp.bfloat16)
    head_out = lax.map(one_head, (query, key_heads, value_heads))
    prefill_out = head_out.transpose(1, 2, 0, 3).reshape(TOKENS, H * VDIM)
    flat_cache = latent_cache.reshape(ROWS * CTX, LAT + ROPE)
    target = place_device * (ROWS_DEV * CTX) + place_slot
    filled = flat_cache.at[target].set(latent).reshape(ROWS, CTX, LAT + ROPE).astype(jnp.float32)
    new_sum = jnp.einsum('srd,dc->src', decode_hidden.astype(jnp.float32), down_weight.astype(jnp.float32))
    new_position = (context_length[None, :] + jnp.arange(STEPS, dtype=jnp.int32)[:, None]).astype(jnp.float32)
    fresh = finalize(new_sum, latent_gain, new_position).astype(jnp.float32)
    step_query = decode_query.reshape(STEPS, ROWS, H, NOPE + ROPE)
    absorbed = jnp.einsum('srhd,chd->srhc', step_query[..., :NOPE].astype(jnp.float32), key_weight.reshape(LAT, H, NOPE).astype(jnp.float32)).astype(jnp.bfloat16)
    full_query = jnp.concatenate([absorbed, step_query[..., NOPE:]], -1).astype(jnp.float32)
    valid = (jnp.arange(CTX, dtype=jnp.int32)[None, :] < context_length[:, None])[:, None, :]
    value_rows = value_weight.reshape(LAT, H, VDIM).astype(jnp.float32)
    results = []
    for step in range(STEPS):
        current = full_query[step]
        recent = fresh[:step + 1]
        older = jnp.where(valid, jnp.einsum('rhc,rkc->rhk', current, filled) * factor, -1e+30)
        newer = jnp.einsum('rhc,trc->rht', current, recent) * factor
        peak = jnp.maximum(lax.optimization_barrier(jnp.max(older, -1)), lax.optimization_barrier(jnp.max(newer, -1)))[..., None]
        older_exp = jnp.where(valid, jnp.exp(older - peak), 0.0)
        newer_exp = jnp.exp(newer - peak)
        total = lax.optimization_barrier(jnp.sum(older_exp, -1)) + lax.optimization_barrier(jnp.sum(newer_exp, -1))
        mixed = jnp.einsum('rhk,rkc->rhc', rounded(older_exp), filled[..., :LAT])
        mixed = mixed + jnp.einsum('rht,trc->rhc', rounded(newer_exp), recent[..., :LAT])
        mixed = (mixed / total[..., None]).astype(jnp.bfloat16).astype(jnp.float32)
        output = jnp.einsum('rhc,chd->rhd', mixed, value_rows).astype(jnp.bfloat16)
        results.append(output.reshape(ROWS, H * VDIM))
    decode_out = jnp.stack(results)
    return (prefill_out, decode_out)
```

```python
import functools

import jax
import jax.numpy as jnp
import numpy as np
from jax import lax
from jax.experimental import pallas as pl
from jax.experimental.pallas import tpu as pltpu
from jax.sharding import PartitionSpec as P

LAT = 512
ROPE = 64
NOPE = 128
VDIM = 128
ROW = 640
TOK = 128
HALF = 64
HEADS = 16
NY, NZ = 4, 8
CHUNK = NZ * TOK
NHP = 8
SETROWS = HEADS * HALF
TQ = 512
SCALE = (NOPE + ROPE) ** (-0.5) * 1.4426950408889634
NEG = -1e30
MESH = pl.DeviceIdType.MESH
f32, bf16, i32 = jnp.float32, jnp.bfloat16, jnp.int32
NT = (((1,), (1,)), ((), ()))

UNITS = [
    [(0, 0), (1, 0), (1, 1), (1, 3), (1, 2)],
    [(0, 1), (1, 1), (0, 0), (1, 0), (1, 2)],
    [(0, 2), (0, 1), (1, 1), (0, 0), (1, 0)],
    [(0, 3), (0, 2), (0, 0), (1, 0), (0, 1)],
]
SET_CODE = [sum(s << (2 * u) for u, (s, c) in enumerate(row)) for row in UNITS]
CHUNK_CODE = [sum(c << (2 * u) for u, (s, c) in enumerate(row)) for row in UNITS]


def pick(y, table):
    return jnp.where(
        y == 0, table[0], jnp.where(y == 1, table[1], jnp.where(y == 2, table[2], table[3]))
    )


def finalize(summed, gain, freq, position):
    content = summed[:, :LAT]
    meansq = jnp.mean(content * content, -1, keepdims=True)
    content = content * lax.rsqrt(meansq + 1e-06) * gain
    tail = summed[:, LAT:]
    lane = lax.broadcasted_iota(i32, tail.shape, 1)
    angle = position * freq
    cosine, sine = jnp.cos(angle), jnp.sin(angle)
    swapped = jnp.where(lane < 32, -pltpu.roll(tail, 96, 1), pltpu.roll(tail, 32, 1))
    rotated = jnp.where(lane < ROPE, tail * cosine + swapped * sine, 0.0)
    return jnp.concatenate([content, rotated], -1).astype(bf16)


def kernel(
    hidden, down, dec_hidden, gain, freq, place_dev, place_slot, dec_query, context, key_w, value_w,
    query, cache,
    out, dec_out,
    kw, vw, q_own, q_far, kept,
    part, part_d, rs, rs_d, lat, meta, fresh,
    qa, qd, m_ref, l_ref, acc, dm, dl, dacc, sbuf, o_far, o_own,
    ld_sem, q_sems, rs_s, rs_r, rd_s, rd_r, ag_s, ag_r,
    mz_s, mz_r, my_s, my_r, z_s, z_r, y_s, y_r, f_s, f_r, sb_s, sb_r, o_sems,
):
    seq = lax.axis_index("seq")
    head = lax.axis_index("head")
    pool = lax.axis_index("pool")
    y, z = seq // NZ, seq % NZ
    hp = head * 4 + pool
    par = (z + head) % 2

    def at_hp(d):
        other = (hp + d) % NHP
        return other, {"head": other // 4, "pool": other % 4}

    def at_z(d):
        return {"seq": y * NZ + (z + d + NZ) % NZ}

    def at_y(d):
        return {"seq": (y + d + NY) % NY * NZ + z}

    partner = {"seq": (NY - 1 - y) * NZ + z}
    sibling = {"head": 1 - head}

    def remote(src, dst, ssem, rsem, dev):
        return pltpu.make_async_remote_copy(
            src_ref=src, dst_ref=dst, send_sem=ssem, recv_sem=rsem, device_id=dev,
            device_id_type=MESH,
        )

    loads = [
        pltpu.make_async_copy(query.at[pl.ds(0, HALF)], q_own, ld_sem.at[0]),
        pltpu.make_async_copy(key_w, kw, ld_sem.at[1]),
        pltpu.make_async_copy(cache, kept, ld_sem.at[2]),
        pltpu.make_async_copy(value_w, vw, ld_sem.at[3]),
    ]
    for copy in loads:
        copy.start()

    barrier = pltpu.get_barrier_semaphore()
    for d in range(1, NHP):
        pl.semaphore_signal(barrier, inc=1, device_id=at_hp(d)[1], device_id_type=MESH)
    for d in range(1, NZ):
        pl.semaphore_signal(barrier, inc=1, device_id=at_z(d), device_id_type=MESH)
    for d in range(1, NY):
        pl.semaphore_signal(barrier, inc=1, device_id=at_y(d), device_id_type=MESH)

    part[:, LAT:] = jnp.zeros((TOK, ROW - LAT), f32)
    part_d[:, LAT:] = jnp.zeros((8, ROW - LAT), f32)
    part[:, : LAT + ROPE] = jnp.dot(hidden[...], down[...], preferred_element_type=f32)
    dh = jnp.concatenate([dec_hidden[0].astype(f32), dec_hidden[1].astype(f32)], 0).astype(bf16)
    part_d[:, : LAT + ROPE] = jnp.dot(dh, down[...], preferred_element_type=f32)
    mine = meta.at[pl.ds(seq, 1)]
    meta[pl.ds(seq, 1), 0:1, :] = place_dev[...].reshape(1, 1, TOK)
    meta[pl.ds(seq, 1), 1:2, :] = place_slot[...].reshape(1, 1, TOK)

    pl.semaphore_wait(barrier, NHP + NZ + NY - 3)

    sends = []

    def go(copy):
        copy.start()
        sends.append(copy)
        return copy

    rs_copies, rd_copies = [], []
    for d in range(1, NHP):
        other, dev = at_hp(d)
        rows = pl.ds(pl.multiple_of(other * 16, 16), 16)
        rs_copies.append(
            go(remote(part.at[rows], rs.at[d - 1], rs_s.at[d - 1], rs_r.at[d - 1], dev))
        )
    mz = [
        go(remote(mine, mine, mz_s.at[d - 1], mz_r.at[d - 1], at_z(d))) for d in range(1, NZ)
    ]
    for d in range(1, NHP):
        rd_copies.append(
            go(remote(part_d, rs_d.at[d - 1], rd_s.at[d - 1], rd_r.at[d - 1], at_hp(d)[1]))
        )
    q_copy = go(remote(query.at[pl.ds(HALF, HALF)], q_far, q_sems.at[0], q_sems.at[1], partner))

    m_ref[...] = jnp.full(m_ref.shape, NEG, f32)
    l_ref[...] = jnp.zeros(l_ref.shape, f32)
    dm[...] = jnp.full(dm.shape, NEG, f32)
    dl[...] = jnp.zeros(dl.shape, f32)
    dacc[...] = jnp.zeros(dacc.shape, f32)

    def clear(i, carry):
        acc[pl.ds(pl.multiple_of(i * 256, 256), 256), :] = jnp.zeros((256, LAT), f32)
        return carry

    lax.fori_loop(0, 2 * SETROWS // 256, clear, 0)

    def absorb(load, dst, base, rows):
        def pair(j, carry):
            col = pl.multiple_of(j * 384, 128)
            t0, t1, t2 = load(col), load(col + 128), load(col + 256)
            lane = lax.broadcasted_iota(i32, t0.shape, 1)
            low = lane < 64
            nopes = (t0, pltpu.roll(jnp.where(low, t2, t1), 64, 1))
            ropes = (jnp.where(low, t1, 0.0), jnp.where(low, pltpu.roll(t2, 64, 1), 0.0))
            both = []
            for k in range(2):
                wcol = pl.multiple_of(j * 256 + k * 128, 128)
                absorbed = lax.dot_general(
                    nopes[k].astype(bf16), kw[:, pl.ds(wcol, 128)], NT, preferred_element_type=f32
                )
                both.append(jnp.concatenate([absorbed, ropes[k]], -1))
            at = pl.multiple_of(base + 2 * j * rows, 2 * rows)
            dst[pl.ds(at, 2 * rows), :] = jnp.concatenate(both, 0).astype(bf16)
            return carry

        lax.fori_loop(0, HEADS // 2, pair, 0)

    loads[0].wait()
    loads[1].wait()
    absorb(lambda c: q_own[:, pl.ds(c, 128)].astype(f32), qa, 0, HALF)
    absorb(
        lambda c: jnp.concatenate(
            [dec_query[0, :, pl.ds(c, 128)], dec_query[1, :, pl.ds(c, 128)]], 0
        ).astype(f32),
        qd, 0, 8,
    )

    for copy in rs_copies:
        copy.wait_recv()
    first = pl.multiple_of(seq * TOK + hp * 16, 16)
    summed = part[pl.ds(pl.multiple_of(hp * 16, 16), 16), :]
    for d in range(1, NHP):
        summed = summed + rs[d - 1]
    position = (first + lax.broadcasted_iota(i32, (16, 1), 0)).astype(f32)
    lat[pl.ds(first, 16), :] = finalize(summed, gain[...], freq[...], position)
    own_rows = lat.at[pl.ds(first, 16)]
    ag = [
        go(remote(own_rows, own_rows, ag_s.at[d - 1], ag_r.at[d - 1], at_hp(d)[1]))
        for d in range(1, NHP)
    ]

    for copy in mz:
        copy.wait_recv()
    plane = meta.at[pl.ds(pl.multiple_of(y * NZ, NZ), NZ)]
    my = [go(remote(plane, plane, my_s.at[d - 1], my_r.at[d - 1], at_y(d))) for d in range(1, NY)]

    for copy in ag:
        copy.wait_recv()

    def block(plane_y, b):
        return lat.at[pl.ds(pl.multiple_of((plane_y * NZ + b) * TOK, TOK), TOK)]

    def z_copy(way, k):
        step = 1 - 2 * way
        b = (z - step * (2 * k + par) + NZ) % NZ
        ref = block(y, b)
        return remote(ref, ref, z_s.at[2 * way + k], z_r.at[2 * way + k], at_z(step))

    def y_copy(way, b):
        ref = block(y, b)
        return remote(
            ref, ref, y_s.at[4 * way + b // 2], y_r.at[4 * way + b // 2], at_y(1 - 2 * way)
        )

    def sib_copy(dist, plane_y, b):
        ref = block(plane_y, b)
        return remote(
            ref, ref, sb_s.at[4 * dist + b // 2], sb_r.at[4 * dist + b // 2], sibling
        )

    def spread(b, to_sibling):
        y_copy(0, b).start()
        y_copy(1, b).start()
        if to_sibling:
            sib_copy(0, y, b).start()

    @pl.when(par == 0)
    def _():
        z_copy(0, 0).start()
        z_copy(1, 0).start()
        spread(z, False)
        z_copy(0, 0).wait_recv()
        z_copy(0, 1).start()
        z_copy(1, 0).wait_recv()
        z_copy(1, 1).start()
        spread((z + 6) % NZ, True)
        spread((z + 2) % NZ, True)
        z_copy(0, 1).wait_recv()
        spread((z + 4) % NZ, True)

    @pl.when(par == 1)
    def _():
        z_copy(0, 0).wait_recv()
        z_copy(0, 0).start()
        z_copy(1, 0).wait_recv()
        z_copy(1, 0).start()
        spread((z + 7) % NZ, True)
        spread((z + 1) % NZ, True)
        z_copy(0, 1).wait_recv()
        z_copy(0, 1).start()
        z_copy(1, 1).wait_recv()
        spread((z + 5) % NZ, True)
        spread((z + 3) % NZ, True)

    q_copy.wait_recv()
    absorb(lambda c: q_far[:, pl.ds(c, 128)].astype(f32), qa, SETROWS, HALF)

    drow = lax.broadcasted_iota(i32, (TOK, 1), 0) % 4
    dstep = lax.broadcasted_iota(i32, (TOK, 1), 0) // 4 % 2

    def decode_update(scores, mask, contents):
        scores = jnp.where(mask, scores * SCALE, NEG)
        m_old = dm[...]
        m_new = jnp.maximum(m_old, jnp.max(scores, -1, keepdims=True))
        alpha = jnp.exp2(m_old - m_new)
        dm[...] = m_new
        expo = jnp.where(mask, jnp.exp2(scores - m_new[:, :1]), 0.0)
        total = dl[...] * alpha
        for j in range(scores.shape[1] // 128):
            total = total + expo[:, 128 * j : 128 * (j + 1)]
        dl[...] = total
        dacc[...] = dacc[...] * alpha[:, :1] + jnp.dot(
            expo.astype(bf16), contents, preferred_element_type=f32
        )

    for copy in rd_copies:
        copy.wait_recv()
    summed = part_d[...]
    for d in range(1, NHP):
        summed = summed + rs_d[d - 1]
    row8 = lax.broadcasted_iota(i32, (8, 1), 0)
    ctx = [context[r] for r in range(4)]
    length = pick(row8 % 4, ctx)
    new_rows = finalize(summed, gain[...], freq[...], (length + row8 // 4).astype(f32))
    fresh[...] = jnp.concatenate([new_rows.astype(f32), jnp.zeros((TOK - 8, ROW), f32)], 0).astype(
        bf16
    )
    key = lax.broadcasted_iota(i32, (1, TOK), 1)
    decode_update(
        lax.dot_general(qd[...], fresh[...], NT, preferred_element_type=f32),
        (key < 8) & (key % 4 == drow) & (key // 4 <= dstep),
        fresh[:, :LAT],
    )

    for copy in my:
        copy.wait_recv()
    counts = jnp.zeros((16, TOK), f32)
    for b in range(NY * NZ):
        device, slot = meta[b, 0:1, :], meta[b, 1:2, :]
        here = device == seq
        high = jnp.where(here, slot // 128, -1)
        low = slot % 128
        one = lax.broadcasted_iota(i32, (16, TOK), 0) == high
        two = lax.broadcasted_iota(i32, (TOK, TOK), 0) == low
        counts = counts + lax.dot_general(
            one.astype(f32).astype(bf16), two.astype(f32).astype(bf16), NT,
            preferred_element_type=f32,
        )
    hi = lax.broadcasted_iota(i32, (16, TOK), 0)
    place = hi % 4 * 128 + lax.broadcasted_iota(i32, (16, TOK), 1)
    live = (place < pick(hi // 4, ctx)) & (counts < 0.5)
    owner = jnp.where(live, hi // 4, -1)
    loads[2].wait()
    for r in range(4):
        keyrow = jnp.concatenate([owner[4 * r + j : 4 * r + j + 1, :] for j in range(4)], 1)
        scores = lax.dot_general(
            qd[:, :LAT], kept[r, :, :LAT], NT, preferred_element_type=f32
        ) + lax.dot_general(
            qd[:, LAT : LAT + ROPE], kept[r, :, LAT:], NT, preferred_element_type=f32
        )
        decode_update(scores, keyrow == drow, kept[r, :, :LAT])

    def decode_chunk(c):
        base = pl.multiple_of(c * CHUNK, CHUNK)
        pieces = []
        for j in range(NZ):
            tile = meta[pl.ds(c * NZ + j, 1), :, :][0]
            pieces.append(jnp.where(tile[0:1] == seq, tile[1:2] // 512, -1))
        keyrow = jnp.concatenate(pieces, 1)
        scores = lax.dot_general(
            qd[...], lat[pl.ds(base, CHUNK), :], NT, preferred_element_type=f32
        )
        decode_update(scores, keyrow == drow, lat[pl.ds(base, CHUNK), :LAT])

    set_code, chunk_code = pick(y, SET_CODE), pick(y, CHUNK_CODE)

    def unit(u):
        return (set_code >> (2 * u)) & 3, (chunk_code >> (2 * u)) & 3

    def rows_of(s, t):
        return pl.ds(pl.multiple_of(s * SETROWS + t * TQ, TQ), TQ)

    def keys_of(c):
        return pl.ds(pl.multiple_of(c * CHUNK, CHUNK), CHUNK)

    def scores_into(slot, s, c, t):
        sbuf[slot] = lax.dot_general(
            qa[rows_of(s, t), :], lat[keys_of(c), :], NT, preferred_element_type=f32
        )

    def attend(slot, s, c, t):
        rows = rows_of(s, t)
        limit = jnp.where(s == 0, y, NY - 1 - y)
        start = jnp.where(c == limit, z * TOK + s * HALF, 1 << 20)
        token = start + lax.broadcasted_iota(i32, (TQ, 1), 0) % HALF
        allowed = lax.broadcasted_iota(i32, (1, CHUNK), 1) <= token
        scores = jnp.where(allowed, sbuf[slot], NEG)
        m_old = m_ref[rows, :]
        m_new = jnp.maximum(m_old, jnp.max(scores, -1, keepdims=True) * SCALE)
        alpha = jnp.exp2(m_old - m_new)
        m_ref[rows, :] = m_new
        expo = jnp.exp2(scores * SCALE - m_new[:, :1])
        total = l_ref[rows, :] * alpha
        for j in range(CHUNK // 128):
            total = total + expo[:, 128 * j : 128 * (j + 1)]
        l_ref[rows, :] = total
        acc[rows, :] = acc[rows, :] * alpha[:, :1] + jnp.dot(
            expo.astype(bf16), lat[keys_of(c), :LAT], preferred_element_type=f32
        )

    def wait_sibling(dist, plane_y):
        for k in range(4):
            b = 2 * k + 1 - head
            if dist == 0:
                pl.when(b != z)(lambda b=b: sib_copy(0, plane_y, b).wait_recv())
            else:
                sib_copy(dist, plane_y, b).wait_recv()

    def near_planes():
        below, above = (y + 3) % NY, (y + 1) % NY
        for way, plane_y in ((0, below), (1, above)):
            for k in range(4):
                b = 2 * k + head
                y_copy(way, b).wait_recv()
                if k % 2 == way:
                    far_copy(way, plane_y, b).start()
                sib_copy(1 + way, plane_y, b).start()
        wait_sibling(1, below)
        wait_sibling(2, above)

    def far_copy(way, plane_y, b):
        ref = block(plane_y, b)
        return remote(ref, ref, f_s.at[b // 2], f_r.at[b // 2], at_y(1 - 2 * way))

    def far_plane():
        plane_y = (y + 2) % NY
        for k in range(4):
            b = 2 * k + head
            far_copy(k % 2, plane_y, b).wait_recv()
            sib_copy(3, plane_y, b).start()
        wait_sibling(3, plane_y)

    wait_sibling(0, y)
    s0, c0 = unit(0)
    scores_into(0, s0, c0, 0)

    def one_unit(u, carry):
        s, c = unit(u)
        sn, cn = unit(u + 1)
        scores_into(1, s, c, 1)
        attend(0, s, c, 0)
        pl.when(((u == 0) & (y >= 2)) | ((u == 1) & (y < 2)))(near_planes)
        pl.when(((u == 2) & (y == 2)) | ((u == 3) & (y != 2)))(far_plane)
        scores_into(0, sn, cn, 0)
        attend(1, s, c, 1)
        decode_chunk((y + jnp.where(u == 0, 0, jnp.where(u == 1, 3, u - 1))) % NY)
        return carry

    lax.fori_loop(0, 4, one_unit, 0)
    s, c = unit(4)
    scores_into(1, s, c, 1)
    attend(0, s, c, 0)
    attend(1, s, c, 1)

    loads[3].wait()

    def project(base, dst):
        def one(j, carry):
            for k in range(2):
                at = pl.ds(pl.multiple_of(base + (2 * j + k) * HALF, HALF), HALF)
                col = pl.ds(pl.multiple_of((2 * j + k) * VDIM, VDIM), VDIM)
                total = jnp.sum(l_ref[at, :], -1, keepdims=True)
                mixed = (acc[at, :] / total).astype(bf16)
                dst[:, col] = jnp.dot(mixed, vw[:, col], preferred_element_type=f32).astype(bf16)
            return carry

        lax.fori_loop(0, HEADS // 2, one, 0)

    project(SETROWS, o_far)
    home = go(remote(o_far, out.at[pl.ds(HALF, HALF)], o_sems.at[0], o_sems.at[1], partner))
    project(0, o_own)
    keep = pltpu.make_async_copy(o_own, out.at[pl.ds(0, HALF)], o_sems.at[2])
    keep.start()
    dmixed = dacc[...] / jnp.sum(dl[...], -1, keepdims=True)
    for h in range(HEADS):
        col = slice(h * VDIM, (h + 1) * VDIM)
        res = jnp.dot(
            dmixed[8 * h : 8 * h + 8].astype(bf16), vw[:, col], preferred_element_type=f32
        ).astype(bf16)
        dec_out[0, :, col] = res[0:4]
        dec_out[1, :, col] = res[4:8]

    for copy in sends:
        copy.wait_send()
    for way in range(2):
        z_copy(way, 0).wait_send()
        for k in range(4):
            y_copy(way, 2 * k + head).wait_send()
    z_copy(0, 1).wait_send()
    pl.when(par == 0)(lambda: z_copy(1, 1).wait_send())
    for k in range(4):
        b = 2 * k + head
        far_copy(k % 2, (y + 3 + 2 * (k % 2)) % NY, b).wait_send()
        pl.when(b != z)(lambda b=b: sib_copy(0, y, b).wait_send())
        sib_copy(1, (y + 3) % NY, b).wait_send()
        sib_copy(2, (y + 1) % NY, b).wait_send()
        sib_copy(3, (y + 2) % NY, b).wait_send()
    keep.wait()
    home.wait_recv()


def on_device(
    prefill_hidden, down_weight, latent_gain, key_weight, value_weight, prefill_query,
    decode_hidden, decode_query, latent_cache, place_device, place_slot, context_length,
):
    half = ROPE // 2
    freq = 10000.0 ** (-(np.arange(128) % half).astype(np.float64) / half)
    freq = jnp.asarray(freq.astype(np.float32)[None])
    vmem = pl.BlockSpec(memory_space=pltpu.VMEM)
    hbm = pl.BlockSpec(memory_space=pl.ANY)
    dma = pltpu.SemaphoreType.DMA
    return pl.pallas_call(
        kernel,
        out_shape=(
            jax.ShapeDtypeStruct((TOK, HEADS * VDIM), bf16),
            jax.ShapeDtypeStruct((2, 4, HEADS * VDIM), bf16),
        ),
        in_specs=[vmem] * 8 + [pl.BlockSpec(memory_space=pltpu.SMEM)] + [hbm] * 4,
        out_specs=(hbm, vmem),
        scratch_shapes=[
            pltpu.VMEM((LAT, HEADS * NOPE), bf16),
            pltpu.VMEM((LAT, HEADS * VDIM), bf16),
            pltpu.VMEM((HALF, HEADS * 192), bf16),
            pltpu.VMEM((HALF, HEADS * 192), bf16),
            pltpu.VMEM((4, 512, LAT + ROPE), bf16),
            pltpu.VMEM((TOK, ROW), f32),
            pltpu.VMEM((8, ROW), f32),
            pltpu.VMEM((NHP - 1, 16, ROW), f32),
            pltpu.VMEM((NHP - 1, 8, ROW), f32),
            pltpu.VMEM((NY * CHUNK, ROW), bf16),
            pltpu.VMEM((NY * NZ, 8, TOK), i32),
            pltpu.VMEM((TOK, ROW), bf16),
            pltpu.VMEM((2 * SETROWS, ROW), bf16),
            pltpu.VMEM((TOK, ROW), bf16),
            pltpu.VMEM((2 * SETROWS, 128), f32),
            pltpu.VMEM((2 * SETROWS, 128), f32),
            pltpu.VMEM((2 * SETROWS, LAT), f32),
            pltpu.VMEM((TOK, 128), f32),
            pltpu.VMEM((TOK, 128), f32),
            pltpu.VMEM((TOK, LAT), f32),
            pltpu.VMEM((2, TQ, CHUNK), f32),
            pltpu.VMEM((HALF, HEADS * VDIM), bf16),
            pltpu.VMEM((HALF, HEADS * VDIM), bf16),
            dma((4,)), dma((2,)),
            dma((7,)), dma((7,)), dma((7,)), dma((7,)), dma((7,)), dma((7,)),
            dma((7,)), dma((7,)), dma((3,)), dma((3,)),
            dma((4,)), dma((4,)), dma((8,)), dma((8,)), dma((4,)), dma((4,)),
            dma((16,)), dma((16,)), dma((3,)),
        ],
        compiler_params=pltpu.CompilerParams(
            collective_id=0, has_side_effects=True, vmem_limit_bytes=56 << 20
        ),
    )(
        prefill_hidden, down_weight, decode_hidden, latent_gain.reshape(1, LAT), freq,
        place_device.reshape(1, TOK), place_slot.reshape(1, TOK), decode_query, context_length,
        key_weight, value_weight, prefill_query, latent_cache,
    )


def solution(mesh):
    in_specs = (
        P("seq", ("head", "pool")),
        P(("head", "pool"), None),
        P(),
        P(None, ("head", "pool")),
        P(None, ("head", "pool")),
        P("seq", ("head", "pool")),
        P(None, "seq", ("head", "pool")),
        P(None, "seq", ("head", "pool")),
        P("seq", None, None),
        P("seq"),
        P("seq"),
        P("seq"),
    )
    out_specs = (P("seq", ("head", "pool")), P(None, "seq", ("head", "pool")))
    return jax.shard_map(
        on_device, mesh=mesh, in_specs=in_specs, out_specs=out_specs, check_vma=False
    )
```

```python
import functools

import jax
import jax.numpy as jnp
import numpy as np
from jax import lax
from jax.experimental import pallas as pl
from jax.experimental.pallas import tpu as pltpu
from jax.sharding import PartitionSpec as P

LAT = 512
ROPE = 64
NOPE = 128
VDIM = 128
ROW = 640
TOK = 128
HALF = 64
HEADS = 16
NY, NZ = 4, 8
CHUNK = NZ * TOK
NHP = 8
OWN, FAR = 2, 5
SETROWS = HEADS * HALF
TQ = 512
SCALE = (NOPE + ROPE) ** (-0.5) * 1.4426950408889634
NEG = -1e30
MESH = pl.DeviceIdType.MESH
f32, bf16, i32 = jnp.float32, jnp.bfloat16, jnp.int32
NT = (((1,), (1,)), ((), ()))

UNITS = [
    [(0, 0), (1, 0), (1, 1), (1, 3), (1, 2)],
    [(0, 1), (1, 1), (0, 0), (1, 0), (1, 2)],
    [(0, 2), (0, 1), (1, 1), (0, 0), (1, 0)],
    [(0, 3), (0, 2), (0, 0), (1, 0), (0, 1)],
]
SET_CODE = [sum(s << (2 * u) for u, (s, c) in enumerate(row)) for row in UNITS]
CHUNK_CODE = [sum(c << (2 * u) for u, (s, c) in enumerate(row)) for row in UNITS]


def pick(y, table):
    return jnp.where(
        y == 0, table[0], jnp.where(y == 1, table[1], jnp.where(y == 2, table[2], table[3]))
    )


def finalize(summed, gain, freq, position):
    content = summed[:, :LAT]
    meansq = jnp.mean(content * content, -1, keepdims=True)
    content = content * lax.rsqrt(meansq + 1e-06) * gain
    tail = summed[:, LAT:]
    lane = lax.broadcasted_iota(i32, tail.shape, 1)
    angle = position * freq
    cosine, sine = jnp.cos(angle), jnp.sin(angle)
    swapped = jnp.where(lane < 32, -pltpu.roll(tail, 96, 1), pltpu.roll(tail, 32, 1))
    rotated = jnp.where(lane < ROPE, tail * cosine + swapped * sine, 0.0)
    return jnp.concatenate([content, rotated], -1).astype(bf16)


def kernel(
    hidden_in, down_in, dec_hidden_in, gain_in, freq_in, dev_in, slot_in, dec_query_in, context,
    key_w, value_w, query, cache,
    out, dec_out,
    hidden, down, dec_hidden, gain, freq, place_dev, place_slot, dec_query,
    kw, vw, q_own, q_far, kept,
    part, part_d, rs, rs_d, lat, meta, fresh,
    qa, qd, m_ref, l_ref, acc, dm, dl, dacc, sbuf, o_far, o_own,
    ld_sem, q_sems, rs_s, rs_r, rd_s, rd_r, mz_s, mz_r, my_s, my_r,
    ax_s, ax_r, fz_s, fz_r, nz_s, nz_r, xf_s, xf_r, yf_s, yf_r, yn_s, yn_r, fw_s, fw_r,
    sb_s, sb_r, o_sems,
):
    seq = lax.axis_index("seq")
    head = lax.axis_index("head")
    pool = lax.axis_index("pool")
    y, z = seq // NZ, seq % NZ
    hp = head * 4 + pool

    def at_hp(d):
        other = (hp + d) % NHP
        return other, {"head": other // 4, "pool": other % 4}

    def at_z(d):
        return {"seq": y * NZ + (z + d + NZ) % NZ}

    def at_y(d):
        return {"seq": (y + d + NY) % NY * NZ + z}

    def at_x(d):
        return {"pool": (pool + d) % 4}

    partner = {"seq": (NY - 1 - y) * NZ + z}
    sibling = {"head": 1 - head}

    def remote(src, dst, ssem, rsem, dev):
        return pltpu.make_async_remote_copy(
            src_ref=src, dst_ref=dst, send_sem=ssem, recv_sem=rsem, device_id=dev,
            device_id_type=MESH,
        )

    first_loads = [
        pltpu.make_async_copy(src, dst, ld_sem.at[4 + i])
        for i, (src, dst) in enumerate(
            (
                (hidden_in, hidden), (down_in, down), (dec_hidden_in, dec_hidden),
                (dev_in, place_dev), (slot_in, place_slot), (gain_in, gain), (freq_in, freq),
                (dec_query_in, dec_query),
            )
        )
    ]
    loads = [
        pltpu.make_async_copy(query.at[pl.ds(0, HALF)], q_own, ld_sem.at[0]),
        pltpu.make_async_copy(key_w, kw, ld_sem.at[1]),
        pltpu.make_async_copy(cache, kept, ld_sem.at[2]),
        pltpu.make_async_copy(value_w, vw, ld_sem.at[3]),
    ]
    for copy in first_loads + loads:
        copy.start()

    barrier = pltpu.get_barrier_semaphore()
    for d in range(1, NHP):
        pl.semaphore_signal(barrier, inc=1, device_id=at_hp(d)[1], device_id_type=MESH)
    for d in range(1, NZ):
        pl.semaphore_signal(barrier, inc=1, device_id=at_z(d), device_id_type=MESH)
    for d in range(1, NY):
        pl.semaphore_signal(barrier, inc=1, device_id=at_y(d), device_id_type=MESH)

    for copy in first_loads:
        copy.wait()
    part[:, LAT:] = jnp.zeros((TOK, ROW - LAT), f32)
    part_d[:, LAT:] = jnp.zeros((8, ROW - LAT), f32)
    part[:, : LAT + ROPE] = lax.dot_general(
        hidden[...], down[...], NT, preferred_element_type=f32
    )
    dh = jnp.concatenate([dec_hidden[0].astype(f32), dec_hidden[1].astype(f32)], 0).astype(bf16)
    part_d[:, : LAT + ROPE] = lax.dot_general(dh, down[...], NT, preferred_element_type=f32)
    mine = meta.at[pl.ds(seq, 1)]
    meta[pl.ds(seq, 1), 0:1, :] = place_dev[...].reshape(1, 1, TOK)
    meta[pl.ds(seq, 1), 1:2, :] = place_slot[...].reshape(1, 1, TOK)

    pl.semaphore_wait(barrier, NHP + NZ + NY - 3)

    sends = []

    def go(copy):
        copy.start()
        sends.append(copy)
        return copy

    rs_copies, rd_copies = [], []
    for d in range(1, NHP):
        other, dev = at_hp(d)
        rows = pl.ds(pl.multiple_of(other * 16, 16), 16)
        rs_copies.append(
            go(remote(part.at[rows], rs.at[d - 1], rs_s.at[d - 1], rs_r.at[d - 1], dev))
        )
    mz = [
        go(remote(mine, mine, mz_s.at[d - 1], mz_r.at[d - 1], at_z(d))) for d in range(1, NZ)
    ]
    q_copy = go(remote(query.at[pl.ds(HALF, HALF)], q_far, q_sems.at[0], q_sems.at[1], partner))

    m_ref[...] = jnp.full(m_ref.shape, NEG, f32)
    l_ref[...] = jnp.zeros(l_ref.shape, f32)
    dm[...] = jnp.full(dm.shape, NEG, f32)
    dl[...] = jnp.zeros(dl.shape, f32)
    dacc[...] = jnp.zeros(dacc.shape, f32)

    def clear(i, carry):
        acc[pl.ds(pl.multiple_of(i * 256, 256), 256), :] = jnp.zeros((256, LAT), f32)
        return carry

    lax.fori_loop(0, 2 * SETROWS // 256, clear, 0)

    def absorb(load, dst, base, rows):
        def pair(j, carry):
            col = pl.multiple_of(j * 384, 128)
            t0, t1, t2 = load(col), load(col + 128), load(col + 256)
            lane = lax.broadcasted_iota(i32, t0.shape, 1)
            low = lane < 64
            nopes = (t0, pltpu.roll(jnp.where(low, t2, t1), 64, 1))
            ropes = (jnp.where(low, t1, 0.0), jnp.where(low, pltpu.roll(t2, 64, 1), 0.0))
            both = []
            for k in range(2):
                wcol = pl.multiple_of(j * 256 + k * 128, 128)
                absorbed = lax.dot_general(
                    nopes[k].astype(bf16), kw[:, pl.ds(wcol, 128)], NT, preferred_element_type=f32
                )
                both.append(jnp.concatenate([absorbed, ropes[k]], -1))
            at = pl.multiple_of(base + 2 * j * rows, 2 * rows)
            dst[pl.ds(at, 2 * rows), :] = jnp.concatenate(both, 0).astype(bf16)
            return carry

        lax.fori_loop(0, HEADS // 2, pair, 0)

    loads[0].wait()
    loads[1].wait()
    absorb(lambda c: q_own[:, pl.ds(c, 128)].astype(f32), qa, 0, HALF)
    absorb(
        lambda c: jnp.concatenate(
            [dec_query[0, :, pl.ds(c, 128)], dec_query[1, :, pl.ds(c, 128)]], 0
        ).astype(f32),
        qd, 0, 8,
    )

    for copy in rs_copies:
        copy.wait_recv()
    first = seq * TOK + hp * 16
    summed = part[pl.ds(pl.multiple_of(hp * 16, 16), 16), :]
    for d in range(1, NHP):
        summed = summed + rs[d - 1]
    position = (first + lax.broadcasted_iota(i32, (16, 1), 0)).astype(f32)
    lat[y, OWN, hp] = finalize(summed, gain[...], freq[...], position)

    half = pl.ds(head * 4, 4)
    own_rows = lat.at[y, OWN, hp]
    ax = [
        go(remote(own_rows, own_rows, ax_s.at[d - 1], ax_r.at[d - 1], at_x(d))) for d in (1, 2, 3)
    ]
    fz = []
    for k, d in enumerate((3, 4, 5)):
        there = lat.at[y, (OWN - d) % NZ, hp]
        fz.append(go(remote(own_rows, there, fz_s.at[k], fz_r.at[k], at_z(d))))
    for d in range(1, NHP):
        rd_copies.append(
            go(remote(part_d, rs_d.at[d - 1], rd_s.at[d - 1], rd_r.at[d - 1], at_hp(d)[1]))
        )

    for copy in ax:
        copy.wait_recv()
    own_half = lat.at[y, OWN, half]
    nz = {}
    for k, d in enumerate((1, -1, 2, -2)):
        there = lat.at[y, OWN - d, half]
        nz[d] = go(remote(own_half, there, nz_s.at[k], nz_r.at[k], at_z(d)))

    def to_planes(i):
        ref = lat.at[y, i, half]
        for w, d in enumerate((1, -1)):
            yn[d].append(go(remote(ref, ref, yn_s.at[5 * w + i], yn_r.at[5 * w + i], at_y(d))))

    yn = {1: [], -1: []}
    to_planes(OWN)

    for copy in mz:
        copy.wait_recv()
    plane = meta.at[pl.ds(pl.multiple_of(y * NZ, NZ), NZ)]
    my = [go(remote(plane, plane, my_s.at[d - 1], my_r.at[d - 1], at_y(d))) for d in range(1, NY)]

    def over_x(dist, plane_y):
        ref = lat.at[plane_y, pl.ds(FAR, 3), hp]
        return [
            go(
                remote(
                    ref, ref, xf_s.at[3 * dist + d - 1], xf_r.at[3 * dist + d - 1], at_x(d)
                )
            )
            for d in (1, 2, 3)
        ]

    for copy in fz:
        copy.wait_recv()
    xf = [over_x(0, y)]
    far_rows = lat.at[y, pl.ds(FAR, 3), hp]
    yf = [go(remote(far_rows, far_rows, yf_s.at[d - 1], yf_r.at[d - 1], at_y(d))) for d in (1, 2, 3)]

    def to_sibling(k, plane_y, start, count):
        ref = lat.at[plane_y, pl.ds(start, count), half]
        return remote(ref, ref, sb_s.at[k], sb_r.at[k], sibling)

    def from_sibling(k, plane_y, start, count):
        to_sibling(k, plane_y, start, count).wait_recv()

    q_copy.wait_recv()
    absorb(lambda c: q_far[:, pl.ds(c, 128)].astype(f32), qa, SETROWS, HALF)

    for d in (1, -1, 2, -2):
        nz[d].wait_recv()
        to_planes(OWN - d)
    to_sibling(0, y, 0, 5).start()
    for d in (1, 2, 3):
        yf[d - 1].wait_recv()
        xf.append(over_x(d, (y - d + NY) % NY))
    for copy in xf[0]:
        copy.wait_recv()
    to_sibling(1, y, FAR, 3).start()

    drow = lax.broadcasted_iota(i32, (TOK, 1), 0) % 4
    dstep = lax.broadcasted_iota(i32, (TOK, 1), 0) // 4 % 2

    def decode_update(scores, mask, contents, dims=(((1,), (0,)), ((), ()))):
        scores = jnp.where(mask, scores * SCALE, NEG)
        m_old = dm[...]
        m_new = jnp.maximum(m_old, jnp.max(scores, -1, keepdims=True))
        alpha = jnp.exp2(m_old - m_new)
        dm[...] = m_new
        expo = jnp.where(mask, jnp.exp2(scores - m_new[:, :1]), 0.0)
        total = dl[...] * alpha
        for j in range(scores.shape[1] // 128):
            total = total + expo[:, 128 * j : 128 * (j + 1)]
        dl[...] = total
        dacc[...] = dacc[...] * alpha[:, :1] + lax.dot_general(
            expo.astype(bf16), contents, dims, preferred_element_type=f32
        )

    for copy in rd_copies:
        copy.wait_recv()
    summed = part_d[...]
    for d in range(1, NHP):
        summed = summed + rs_d[d - 1]
    row8 = lax.broadcasted_iota(i32, (8, 1), 0)
    ctx = [context[r] for r in range(4)]
    length = pick(row8 % 4, ctx)
    new_rows = finalize(summed, gain[...], freq[...], (length + row8 // 4).astype(f32))
    fresh[...] = jnp.concatenate([new_rows.astype(f32), jnp.zeros((TOK - 8, ROW), f32)], 0).astype(
        bf16
    )
    key = lax.broadcasted_iota(i32, (1, TOK), 1)
    decode_update(
        lax.dot_general(qd[...], fresh[...], NT, preferred_element_type=f32),
        (key < 8) & (key % 4 == drow) & (key // 4 <= dstep),
        fresh[:, :LAT],
    )

    for copy in my:
        copy.wait_recv()
    counts = jnp.zeros((16, TOK), f32)
    for b in range(NY * NZ):
        device, slot = meta[b, 0:1, :], meta[b, 1:2, :]
        here = device == seq
        high = jnp.where(here, slot // 128, -1)
        low = slot % 128
        one = lax.broadcasted_iota(i32, (16, TOK), 0) == high
        two = lax.broadcasted_iota(i32, (TOK, TOK), 0) == low
        counts = counts + lax.dot_general(
            one.astype(f32).astype(bf16), two.astype(f32).astype(bf16), NT,
            preferred_element_type=f32,
        )
    hi = lax.broadcasted_iota(i32, (16, TOK), 0)
    place = hi % 4 * 128 + lax.broadcasted_iota(i32, (16, TOK), 1)
    live = (place < pick(hi // 4, ctx)) & (counts < 0.5)
    owner = jnp.where(live, hi // 4, -1)
    loads[2].wait()
    for r in range(4):
        keyrow = jnp.concatenate([owner[4 * r + j : 4 * r + j + 1, :] for j in range(4)], 1)
        scores = jnp.dot(qd[:, :LAT], kept[r, :LAT], preferred_element_type=f32) + jnp.dot(
            qd[:, LAT : LAT + ROPE], kept[r, LAT:], preferred_element_type=f32
        )
        decode_update(scores, keyrow == drow, kept[r, :LAT], NT)

    def decode_chunk(c):
        pieces = []
        for j in range(NZ):
            tile = meta[pl.ds(c * NZ + (z + j + 6) % NZ, 1), :, :][0]
            pieces.append(jnp.where(tile[0:1] == seq, tile[1:2] // 512, -1))
        keyrow = jnp.concatenate(pieces, 1)
        scores = lax.dot_general(
            qd[...], lat[c].reshape(CHUNK, ROW), NT, preferred_element_type=f32
        )
        decode_update(scores, keyrow == drow, lat[c, :, :, :, :LAT].reshape(CHUNK, LAT))

    set_code, chunk_code = pick(y, SET_CODE), pick(y, CHUNK_CODE)

    def unit(u):
        return (set_code >> (2 * u)) & 3, (chunk_code >> (2 * u)) & 3

    def rows_of(s, t):
        return pl.ds(pl.multiple_of(s * SETROWS + t * TQ, TQ), TQ)

    def scores_into(slot, s, c, t):
        sbuf[slot] = lax.dot_general(
            qa[rows_of(s, t), :], lat[c].reshape(CHUNK, ROW), NT, preferred_element_type=f32
        )

    def attend(slot, s, c, t):
        rows = rows_of(s, t)
        limit = jnp.where(s == 0, y, NY - 1 - y)
        start = jnp.where(c == limit, z * TOK + s * HALF, 1 << 20)
        token = start + lax.broadcasted_iota(i32, (TQ, 1), 0) % HALF
        key = (lax.broadcasted_iota(i32, (1, CHUNK), 1) + (z + 6) * TOK) & (CHUNK - 1)
        allowed = key <= token
        scores = jnp.where(allowed, sbuf[slot], NEG)
        m_old = m_ref[rows, :]
        m_new = jnp.maximum(m_old, jnp.max(scores, -1, keepdims=True) * SCALE)
        alpha = jnp.exp2(m_old - m_new)
        m_ref[rows, :] = m_new
        expo = jnp.exp2(scores * SCALE - m_new[:, :1])
        total = l_ref[rows, :] * alpha
        for j in range(CHUNK // 128):
            total = total + expo[:, 128 * j : 128 * (j + 1)]
        l_ref[rows, :] = total
        acc[rows, :] = acc[rows, :] * alpha[:, :1] + jnp.dot(
            expo.astype(bf16), lat[c, :, :, :, :LAT].reshape(CHUNK, LAT), preferred_element_type=f32
        )

    below, above, across = (y + 3) % NY, (y + 1) % NY, (y + 2) % NY

    def forward(w):
        ref = lat.at[(below, above)[w], pl.ds(2 * w, 2 + w), half]
        return remote(ref, ref, fw_s.at[w], fw_r.at[w], at_y(1 - 2 * w))

    def forwarded(w):
        ref = lat.at[across, pl.ds(2 * w, 2 + w), half]
        return remote(ref, ref, fw_s.at[w], fw_r.at[w], at_y(1 - 2 * w))

    def near_planes():
        for w, (d, plane_y) in enumerate(((1, below), (-1, above))):
            for copy in yn[d]:
                copy.wait_recv()
            forward(w).start()
            to_sibling(2 + 2 * w, plane_y, 0, 5).start()
        for w, (dist, plane_y) in enumerate(((1, below), (3, above))):
            for copy in xf[dist]:
                copy.wait_recv()
            to_sibling(3 + 2 * w, plane_y, FAR, 3).start()
        for w, plane_y in enumerate((below, above)):
            from_sibling(2 + 2 * w, plane_y, 0, 5)
            from_sibling(3 + 2 * w, plane_y, FAR, 3)

    def far_plane():
        for w in range(2):
            forwarded(w).wait_recv()
        for copy in xf[2]:
            copy.wait_recv()
        to_sibling(6, across, 0, NZ).start()
        from_sibling(6, across, 0, NZ)

    from_sibling(0, y, 0, 5)
    from_sibling(1, y, FAR, 3)
    s0, c0 = unit(0)
    scores_into(0, s0, c0, 0)

    def one_unit(u, carry):
        s, c = unit(u)
        sn, cn = unit(u + 1)
        scores_into(1, s, c, 1)
        attend(0, s, c, 0)
        pl.when(((u == 0) & (y >= 2)) | ((u == 1) & (y < 2)))(near_planes)
        pl.when(((u == 2) & (y == 2)) | ((u == 3) & (y != 2)))(far_plane)
        scores_into(0, sn, cn, 0)
        attend(1, s, c, 1)
        decode_chunk((y + jnp.where(u == 0, 0, jnp.where(u == 1, 3, u - 1))) % NY)
        return carry

    lax.fori_loop(0, 4, one_unit, 0)
    s, c = unit(4)
    scores_into(1, s, c, 1)
    attend(0, s, c, 0)
    attend(1, s, c, 1)

    loads[3].wait()

    def project(base, dst):
        def one(j, carry):
            for k in range(2):
                at = pl.ds(pl.multiple_of(base + (2 * j + k) * HALF, HALF), HALF)
                col = pl.ds(pl.multiple_of((2 * j + k) * VDIM, VDIM), VDIM)
                total = jnp.sum(l_ref[at, :], -1, keepdims=True)
                mixed = (acc[at, :] / total).astype(bf16)
                dst[:, col] = jnp.dot(mixed, vw[:, col], preferred_element_type=f32).astype(bf16)
            return carry

        lax.fori_loop(0, HEADS // 2, one, 0)

    project(SETROWS, o_far)
    home = go(remote(o_far, out.at[pl.ds(HALF, HALF)], o_sems.at[0], o_sems.at[1], partner))
    project(0, o_own)
    keep = pltpu.make_async_copy(o_own, out.at[pl.ds(0, HALF)], o_sems.at[2])
    keep.start()
    dmixed = dacc[...] / jnp.sum(dl[...], -1, keepdims=True)
    for h in range(HEADS):
        col = slice(h * VDIM, (h + 1) * VDIM)
        res = jnp.dot(
            dmixed[8 * h : 8 * h + 8].astype(bf16), vw[:, col], preferred_element_type=f32
        ).astype(bf16)
        dec_out[0, :, col] = res[0:4]
        dec_out[1, :, col] = res[4:8]

    for copy in sends:
        copy.wait_send()
    for w in range(2):
        forward(w).wait_send()
        to_sibling(2 + 2 * w, (below, above)[w], 0, 5).wait_send()
        to_sibling(3 + 2 * w, (below, above)[w], FAR, 3).wait_send()
    to_sibling(0, y, 0, 5).wait_send()
    to_sibling(1, y, FAR, 3).wait_send()
    to_sibling(6, across, 0, NZ).wait_send()
    keep.wait()
    home.wait_recv()


def on_device(
    prefill_hidden, down_weight, latent_gain, key_weight, value_weight, prefill_query,
    decode_hidden, decode_query, latent_cache, place_device, place_slot, context_length,
):
    half = ROPE // 2
    freq = 10000.0 ** (-(np.arange(128) % half).astype(np.float64) / half)
    freq = jnp.asarray(freq.astype(np.float32)[None])
    vmem = pl.BlockSpec(memory_space=pltpu.VMEM)
    hbm = pl.BlockSpec(memory_space=pl.ANY)
    dma = pltpu.SemaphoreType.DMA
    return pl.pallas_call(
        kernel,
        out_shape=(
            jax.ShapeDtypeStruct((TOK, HEADS * VDIM), bf16),
            jax.ShapeDtypeStruct((2, 4, HEADS * VDIM), bf16),
        ),
        in_specs=[hbm] * 8 + [pl.BlockSpec(memory_space=pltpu.SMEM)] + [hbm] * 4,
        out_specs=(hbm, vmem),
        scratch_shapes=[
            pltpu.VMEM((TOK, 896), bf16),
            pltpu.VMEM((LAT + ROPE, 896), bf16),
            pltpu.VMEM((2, 4, 896), bf16),
            pltpu.VMEM((1, LAT), f32),
            pltpu.VMEM((1, 128), f32),
            pltpu.VMEM((1, TOK), i32),
            pltpu.VMEM((1, TOK), i32),
            pltpu.VMEM((2, 4, HEADS * 192), bf16),
            pltpu.VMEM((LAT, HEADS * NOPE), bf16),
            pltpu.VMEM((LAT, HEADS * VDIM), bf16),
            pltpu.VMEM((HALF, HEADS * 192), bf16),
            pltpu.VMEM((HALF, HEADS * 192), bf16),
            pltpu.VMEM((4, LAT + ROPE, 512), bf16),
            pltpu.VMEM((TOK, ROW), f32),
            pltpu.VMEM((8, ROW), f32),
            pltpu.VMEM((NHP - 1, 16, ROW), f32),
            pltpu.VMEM((NHP - 1, 8, ROW), f32),
            pltpu.VMEM((NY, NZ, NHP, 16, ROW), bf16),
            pltpu.VMEM((NY * NZ, 8, TOK), i32),
            pltpu.VMEM((TOK, ROW), bf16),
            pltpu.VMEM((2 * SETROWS, ROW), bf16),
            pltpu.VMEM((TOK, ROW), bf16),
            pltpu.VMEM((2 * SETROWS, 128), f32),
            pltpu.VMEM((2 * SETROWS, 128), f32),
            pltpu.VMEM((2 * SETROWS, LAT), f32),
            pltpu.VMEM((TOK, 128), f32),
            pltpu.VMEM((TOK, 128), f32),
            pltpu.VMEM((TOK, LAT), f32),
            pltpu.VMEM((2, TQ, CHUNK), f32),
            pltpu.VMEM((HALF, HEADS * VDIM), bf16),
            pltpu.VMEM((HALF, HEADS * VDIM), bf16),
            dma((12,)), dma((2,)), dma((7,)), dma((7,)), dma((7,)), dma((7,)),
            dma((7,)), dma((7,)), dma((3,)), dma((3,)),
            dma((3,)), dma((3,)), dma((3,)), dma((3,)), dma((4,)), dma((4,)),
            dma((12,)), dma((12,)), dma((3,)), dma((3,)), dma((10,)), dma((10,)),
            dma((2,)), dma((2,)), dma((7,)), dma((7,)), dma((3,)),
        ],
        compiler_params=pltpu.CompilerParams(
            collective_id=0, has_side_effects=True, vmem_limit_bytes=56 << 20
        ),
    )(
        prefill_hidden, down_weight.T, decode_hidden, latent_gain.reshape(1, LAT), freq,
        place_device.reshape(1, TOK), place_slot.reshape(1, TOK), decode_query, context_length,
        key_weight, value_weight, prefill_query, latent_cache.transpose(0, 2, 1),
    )


def solution(mesh):
    in_specs = (
        P("seq", ("head", "pool")),
        P(("head", "pool"), None),
        P(),
        P(None, ("head", "pool")),
        P(None, ("head", "pool")),
        P("seq", ("head", "pool")),
        P(None, "seq", ("head", "pool")),
        P(None, "seq", ("head", "pool")),
        P("seq", None, None),
        P("seq"),
        P("seq"),
        P("seq"),
    )
    out_specs = (P("seq", ("head", "pool")), P(None, "seq", ("head", "pool")))
    return jax.shard_map(
        on_device, mesh=mesh, in_specs=in_specs, out_specs=out_specs, check_vma=False
    )
```

```python
import functools

import jax
import jax.numpy as jnp
import numpy as np
from jax import lax
from jax.experimental import pallas as pl
from jax.experimental.pallas import tpu as pltpu
from jax.sharding import PartitionSpec as P

LAT = 512
ROPE = 64
NOPE = 128
VDIM = 128
ROW = 640
TOK = 128
HEADS = 16
NY, NZ = 4, 8
CHUNK = NZ * TOK
NHP = 8
OWN, FAR = 2, 5
TQ = 512
GUEST = 4
GUEST_COL = 12
SCALE = (NOPE + ROPE) ** (-0.5) * 1.4426950408889634
NEG = -1e30
MESH = pl.DeviceIdType.MESH
f32, bf16, i32 = jnp.float32, jnp.bfloat16, jnp.int32
NT = (((1,), (1,)), ((), ()))

STEPS = [
    [(0, 0), (1, 0), (2, 0), (3, 0), (0, 0), (0, 1), (0, 3), (0, 2)],
    [(t, c) for c in (1, 0) for t in range(4)],
    [(t, c) for c in (2, 1, 0) for t in range(4)],
    [(t, c) for c in (3, 2, 0, 1) for t in range(3)],
]
TILE_CODE = [sum(t << (2 * n) for n, (t, c) in enumerate(row)) for row in STEPS]
CHUNK_CODE = [sum(c << (2 * n) for n, (t, c) in enumerate(row)) for row in STEPS]


def pick(y, table):
    return jnp.where(
        y == 0, table[0], jnp.where(y == 1, table[1], jnp.where(y == 2, table[2], table[3]))
    )


def finalize(summed, gain, freq, position):
    content = summed[:, :LAT]
    meansq = jnp.mean(content * content, -1, keepdims=True)
    content = content * lax.rsqrt(meansq + 1e-06) * gain
    tail = summed[:, LAT:]
    lane = lax.broadcasted_iota(i32, tail.shape, 1)
    angle = position * freq
    cosine, sine = jnp.cos(angle), jnp.sin(angle)
    swapped = jnp.where(lane < 32, -pltpu.roll(tail, 96, 1), pltpu.roll(tail, 32, 1))
    rotated = jnp.where(lane < ROPE, tail * cosine + swapped * sine, 0.0)
    return jnp.concatenate([content, rotated], -1).astype(bf16)


def kernel(
    hidden_in, down_in, dec_hidden_in, gain_in, freq_in, dev_in, slot_in, dec_query_in, context,
    key_w, value_w, query, cache,
    out, dec_out,
    hidden, down, dec_hidden, gain, freq, place_dev, place_slot, dec_query,
    kw, vw, q_own, q_far, kept,
    part, part_d, rs, rs_d, lat, meta, fresh,
    qa, qd, m_ref, l_ref, acc, dm, dl, dacc, sbuf, o_own, o_guest,
    ld_sem, q_sems, rs_s, rs_r, rd_s, rd_r, mz_s, mz_r, my_s, my_r,
    ax_s, ax_r, fz_s, fz_r, nz_s, nz_r, xf_s, xf_r, yf_s, yf_r, yn_s, yn_r, yo_s, yo_r, zs_s, zs_r,
    sb_s, sb_r, o_sems,
):
    seq = lax.axis_index("seq")
    head = lax.axis_index("head")
    pool = lax.axis_index("pool")
    y, z = seq // NZ, seq % NZ
    hp = head * 4 + pool

    def at_hp(d):
        other = (hp + d) % NHP
        return other, {"head": other // 4, "pool": other % 4}

    def at_z(d):
        return {"seq": y * NZ + (z + d + NZ) % NZ}

    def at_y(d):
        return {"seq": (y + d + NY) % NY * NZ + z}

    def at_x(d):
        return {"pool": (pool + d) % 4}

    partner = {"seq": (NY - 1 - y) * NZ + z}
    sibling = {"head": 1 - head}

    def remote(src, dst, ssem, rsem, dev):
        return pltpu.make_async_remote_copy(
            src_ref=src, dst_ref=dst, send_sem=ssem, recv_sem=rsem, device_id=dev,
            device_id_type=MESH,
        )

    first_loads = [
        pltpu.make_async_copy(src, dst, ld_sem.at[4 + i])
        for i, (src, dst) in enumerate(
            (
                (hidden_in, hidden), (down_in, down), (dec_hidden_in, dec_hidden),
                (dev_in, place_dev), (slot_in, place_slot), (gain_in, gain), (freq_in, freq),
                (dec_query_in, dec_query),
            )
        )
    ]
    loads = [
        pltpu.make_async_copy(query, q_own, ld_sem.at[0]),
        pltpu.make_async_copy(key_w, kw, ld_sem.at[1]),
        pltpu.make_async_copy(cache, kept, ld_sem.at[2]),
        pltpu.make_async_copy(value_w, vw, ld_sem.at[3]),
    ]
    for copy in first_loads + loads:
        copy.start()

    barrier = pltpu.get_barrier_semaphore()
    for d in range(1, NHP):
        pl.semaphore_signal(barrier, inc=1, device_id=at_hp(d)[1], device_id_type=MESH)
    for d in range(1, NZ):
        pl.semaphore_signal(barrier, inc=1, device_id=at_z(d), device_id_type=MESH)
    for d in range(1, NY):
        pl.semaphore_signal(barrier, inc=1, device_id=at_y(d), device_id_type=MESH)

    for copy in first_loads:
        copy.wait()
    part[:, LAT:] = jnp.zeros((TOK, ROW - LAT), f32)
    part_d[:, LAT:] = jnp.zeros((8, ROW - LAT), f32)
    part[:, : LAT + ROPE] = lax.dot_general(
        hidden[...], down[...], NT, preferred_element_type=f32
    )
    dh = jnp.concatenate([dec_hidden[0].astype(f32), dec_hidden[1].astype(f32)], 0).astype(bf16)
    part_d[:, : LAT + ROPE] = lax.dot_general(dh, down[...], NT, preferred_element_type=f32)
    mine = meta.at[pl.ds(seq, 1)]
    meta[pl.ds(seq, 1), 0:1, :] = place_dev[...].reshape(1, 1, TOK)
    meta[pl.ds(seq, 1), 1:2, :] = place_slot[...].reshape(1, 1, TOK)

    pl.semaphore_wait(barrier, NHP + NZ + NY - 3)

    sends = []

    def go(copy):
        copy.start()
        sends.append(copy)
        return copy

    rs_copies, rd_copies = [], []
    for d in range(1, NHP):
        other, dev = at_hp(d)
        rows = pl.ds(pl.multiple_of(other * 16, 16), 16)
        rs_copies.append(
            go(remote(part.at[rows], rs.at[d - 1], rs_s.at[d - 1], rs_r.at[d - 1], dev))
        )
    mz = [
        go(remote(mine, mine, mz_s.at[d - 1], mz_r.at[d - 1], at_z(d))) for d in range(1, NZ)
    ]
    q_copy = remote(
        query.at[:, pl.ds(GUEST_COL * 192, 768)], q_far, q_sems.at[0], q_sems.at[1], partner
    )
    pl.when(y == 3)(lambda: q_copy.start())

    m_ref[...] = jnp.full(m_ref.shape, NEG, f32)
    l_ref[...] = jnp.zeros(l_ref.shape, f32)
    dm[...] = jnp.full(dm.shape, NEG, f32)
    dl[...] = jnp.zeros(dl.shape, f32)
    dacc[...] = jnp.zeros(dacc.shape, f32)

    def clear(i, carry):
        acc[pl.ds(pl.multiple_of(i * 256, 256), 256), :] = jnp.zeros((256, LAT), f32)
        return carry

    lax.fori_loop(0, 5 * TQ // 256, clear, 0)

    def absorb(load, dst, base, rows, first=0, last=HEADS // 2):
        def pair(j, carry):
            col = pl.multiple_of(j * 384, 128)
            t0, t1, t2 = load(col), load(col + 128), load(col + 256)
            lane = lax.broadcasted_iota(i32, t0.shape, 1)
            low = lane < 64
            nopes = (t0, pltpu.roll(jnp.where(low, t2, t1), 64, 1))
            ropes = (jnp.where(low, t1, 0.0), jnp.where(low, pltpu.roll(t2, 64, 1), 0.0))
            both = []
            for k in range(2):
                wcol = pl.multiple_of((first + j) * 256 + k * 128, 128)
                absorbed = lax.dot_general(
                    nopes[k].astype(bf16), kw[:, pl.ds(wcol, 128)], NT, preferred_element_type=f32
                )
                both.append(jnp.concatenate([absorbed, ropes[k]], -1))
            at = pl.multiple_of(base + 2 * j * rows, 2 * rows)
            dst[pl.ds(at, 2 * rows), :] = jnp.concatenate(both, 0).astype(bf16)
            return carry

        lax.fori_loop(0, last - first, pair, 0)

    loads[0].wait()
    loads[1].wait()
    absorb(lambda c: q_own[:, pl.ds(c, 128)].astype(f32), qa, 0, TOK)
    absorb(
        lambda c: jnp.concatenate(
            [dec_query[0, :, pl.ds(c, 128)], dec_query[1, :, pl.ds(c, 128)]], 0
        ).astype(f32),
        qd, 0, 8,
    )

    for copy in rs_copies:
        copy.wait_recv()
    first = seq * TOK + hp * 16
    summed = part[pl.ds(pl.multiple_of(hp * 16, 16), 16), :]
    for d in range(1, NHP):
        summed = summed + rs[d - 1]
    position = (first + lax.broadcasted_iota(i32, (16, 1), 0)).astype(f32)
    lat[y, OWN, hp] = finalize(summed, gain[...], freq[...], position)

    half = pl.ds(head * 4, 4)
    own_rows = lat.at[y, OWN, hp]
    ax = [
        go(remote(own_rows, own_rows, ax_s.at[d - 1], ax_r.at[d - 1], at_x(d))) for d in (1, 2, 3)
    ]
    fz = []
    for k, d in enumerate((3, 4, 5)):
        there = lat.at[y, (OWN - d) % NZ, hp]
        fz.append(go(remote(own_rows, there, fz_s.at[k], fz_r.at[k], at_z(d))))
    for d in range(1, NHP):
        rd_copies.append(
            go(remote(part_d, rs_d.at[d - 1], rd_s.at[d - 1], rd_r.at[d - 1], at_hp(d)[1]))
        )

    for copy in ax:
        copy.wait_recv()
    own_half = lat.at[y, OWN, half]
    nz = {}
    for k, d in enumerate((1, -1, 2, -2)):
        there = lat.at[y, OWN - d, half]
        nz[d] = go(remote(own_half, there, nz_s.at[k], nz_r.at[k], at_z(d)))

    yo = {}
    for k, d in enumerate((1, -1, 2)):
        yo[d] = go(remote(own_half, own_half, yo_s.at[k], yo_r.at[k], at_y(d)))

    below, above, across = (y + 3) % NY, (y + 1) % NY, (y + 2) % NY

    def along_z(k, plane_y, d):
        there = lat.at[plane_y, OWN - d, half]
        return go(
            remote(lat.at[plane_y, OWN, half], there, zs_s.at[k], zs_r.at[k], at_z(d))
        )

    yn = {1: [], -1: []}

    def to_planes(i):
        ref = lat.at[y, i, half]
        for w, d in enumerate((1, -1)):
            k = 2 * w + i // 4
            yn[d].append(go(remote(ref, ref, yn_s.at[k], yn_r.at[k], at_y(d))))

    for copy in mz:
        copy.wait_recv()
    plane = meta.at[pl.ds(pl.multiple_of(y * NZ, NZ), NZ)]
    my = [go(remote(plane, plane, my_s.at[d - 1], my_r.at[d - 1], at_y(d))) for d in range(1, NY)]

    def over_x(dist, plane_y):
        ref = lat.at[plane_y, pl.ds(FAR, 3), hp]
        return [
            go(
                remote(
                    ref, ref, xf_s.at[3 * dist + d - 1], xf_r.at[3 * dist + d - 1], at_x(d)
                )
            )
            for d in (1, 2, 3)
        ]

    for copy in fz:
        copy.wait_recv()
    xf = [over_x(0, y)]
    far_rows = lat.at[y, pl.ds(FAR, 3), hp]
    yf = [go(remote(far_rows, far_rows, yf_s.at[d - 1], yf_r.at[d - 1], at_y(d))) for d in (1, 2, 3)]

    def to_sibling(k, plane_y, start, count):
        ref = lat.at[plane_y, pl.ds(start, count), half]
        return remote(ref, ref, sb_s.at[k], sb_r.at[k], sibling)

    def from_sibling(k, plane_y, start, count):
        to_sibling(k, plane_y, start, count).wait_recv()

    ctx = [context[r] for r in range(4)]
    drow = lax.broadcasted_iota(i32, (TOK, 1), 0) % 4
    dstep = lax.broadcasted_iota(i32, (TOK, 1), 0) // 4 % 2

    def decode_update(scores, mask, contents, dims=(((1,), (0,)), ((), ()))):
        scores = jnp.where(mask, scores * SCALE, NEG)
        m_old = dm[...]
        m_new = jnp.maximum(m_old, jnp.max(scores, -1, keepdims=True))
        alpha = jnp.exp2(m_old - m_new)
        dm[...] = m_new
        expo = jnp.where(mask, jnp.exp2(scores - m_new[:, :1]), 0.0)
        total = dl[...] * alpha
        for j in range(scores.shape[1] // 128):
            total = total + expo[:, 128 * j : 128 * (j + 1)]
        dl[...] = total
        dacc[...] = dacc[...] * alpha[:, :1] + lax.dot_general(
            expo.astype(bf16), contents, dims, preferred_element_type=f32
        )

    @pl.when(y == 0)
    def _():
        q_copy.wait_recv()
        absorb(lambda c: q_far[:, pl.ds(c, 128)].astype(f32), qa, GUEST * TQ, TOK, GUEST_COL // 2)

    for copy in my:
        copy.wait_recv()
    counts = jnp.zeros((16, TOK), f32)
    for b in range(NY * NZ):
        device, slot = meta[b, 0:1, :], meta[b, 1:2, :]
        here = device == seq
        high = jnp.where(here, slot // 128, -1)
        low = slot % 128
        one = lax.broadcasted_iota(i32, (16, TOK), 0) == high
        two = lax.broadcasted_iota(i32, (TOK, TOK), 0) == low
        counts = counts + lax.dot_general(
            one.astype(f32).astype(bf16), two.astype(f32).astype(bf16), NT,
            preferred_element_type=f32,
        )
    hi = lax.broadcasted_iota(i32, (16, TOK), 0)
    place = hi % 4 * 128 + lax.broadcasted_iota(i32, (16, TOK), 1)
    live = (place < pick(hi // 4, ctx)) & (counts < 0.5)
    owner = jnp.where(live, hi // 4, -1)
    loads[2].wait()

    def kept_rows(r):
        keyrow = jnp.concatenate([owner[4 * r + j : 4 * r + j + 1, :] for j in range(4)], 1)
        scores = jnp.dot(qd[:, :LAT], kept[r, :LAT], preferred_element_type=f32) + jnp.dot(
            qd[:, LAT : LAT + ROPE], kept[r, LAT:], preferred_element_type=f32
        )
        decode_update(scores, keyrow == drow, kept[r, :LAT], NT)

    yo[1].wait_recv()
    zs_below = [along_z(k, below, d) for k, d in enumerate((1, -1))]
    yo[-1].wait_recv()
    zs_above = [along_z(2 + k, above, d) for k, d in enumerate((1, -1))]
    for d in (1, -1):
        nz[d].wait_recv()
    to_sibling(0, y, 1, 3).start()
    yo[2].wait_recv()
    zs_across = [along_z(4 + k, across, d) for k, d in enumerate((1, -1, 2, -2))]
    kept_rows(0)
    for d in (2, -2):
        nz[d].wait_recv()
        to_planes(OWN - d)
    to_sibling(1, y, 0, 1).start()
    to_sibling(2, y, 4, 1).start()
    kept_rows(1)
    for d in (1, 2, 3):
        yf[d - 1].wait_recv()
        xf.append(over_x(d, (y - d + NY) % NY))
    for copy in xf[0]:
        copy.wait_recv()
    to_sibling(3, y, FAR, 3).start()
    def decode_rest():
        kept_rows(2)
        kept_rows(3)

        for copy in rd_copies:
            copy.wait_recv()
        summed = part_d[...]
        for d in range(1, NHP):
            summed = summed + rs_d[d - 1]
        row8 = lax.broadcasted_iota(i32, (8, 1), 0)
        length = pick(row8 % 4, ctx)
        new_rows = finalize(summed, gain[...], freq[...], (length + row8 // 4).astype(f32))
        fresh[...] = jnp.concatenate([new_rows.astype(f32), jnp.zeros((TOK - 8, ROW), f32)], 0).astype(
            bf16
        )
        key = lax.broadcasted_iota(i32, (1, TOK), 1)
        decode_update(
            lax.dot_general(qd[...], fresh[...], NT, preferred_element_type=f32),
            (key < 8) & (key % 4 == drow) & (key // 4 <= dstep),
            fresh[:, :LAT],
        )

    def decode_chunk(c):
        pieces = []
        for j in range(NZ):
            tile = meta[pl.ds(c * NZ + (z + j + 6) % NZ, 1), :, :][0]
            pieces.append(jnp.where(tile[0:1] == seq, tile[1:2] // 512, -1))
        keyrow = jnp.concatenate(pieces, 1)
        scores = lax.dot_general(
            qd[...], lat[c].reshape(CHUNK, ROW), NT, preferred_element_type=f32
        )
        decode_update(scores, keyrow == drow, lat[c, :, :, :, :LAT].reshape(CHUNK, LAT))

    tile_code, chunk_code = pick(y, TILE_CODE), pick(y, CHUNK_CODE)

    def step_of(n):
        tile = jnp.where((y == 0) & (n >= 4), GUEST, (tile_code >> (2 * n)) & 3)
        return tile, (chunk_code >> (2 * n)) & 3

    def rows_of(tile):
        return pl.ds(pl.multiple_of(tile * TQ, TQ), TQ)

    def scores_into(slot, n):
        tile, c = step_of(n)
        sbuf[slot] = lax.dot_general(
            qa[rows_of(tile), :], lat[c].reshape(CHUNK, ROW), NT, preferred_element_type=f32
        )

    def attend(slot, n):
        tile, c = step_of(n)
        rows = rows_of(tile)
        limit = jnp.where(tile == GUEST, 3, y)
        start = jnp.where(c == limit, z * TOK, 1 << 20)
        token = start + lax.broadcasted_iota(i32, (TQ, 1), 0) % TOK
        key = (lax.broadcasted_iota(i32, (1, CHUNK), 1) + (z + 6) * TOK) & (CHUNK - 1)
        allowed = key <= token
        scores = jnp.where(allowed, sbuf[slot], NEG)
        m_old = m_ref[rows, :]
        m_new = jnp.maximum(m_old, jnp.max(scores, -1, keepdims=True) * SCALE)
        alpha = jnp.exp2(m_old - m_new)
        m_ref[rows, :] = m_new
        expo = jnp.exp2(scores * SCALE - m_new[:, :1])
        total = l_ref[rows, :] * alpha
        for j in range(CHUNK // 128):
            total = total + expo[:, 128 * j : 128 * (j + 1)]
        l_ref[rows, :] = total
        acc[rows, :] = acc[rows, :] * alpha[:, :1] + jnp.dot(
            expo.astype(bf16), lat[c, :, :, :, :LAT].reshape(CHUNK, LAT), preferred_element_type=f32
        )

    def near_arrive():
        for w, (plane_y, spread) in enumerate(((below, zs_below), (above, zs_above))):
            for copy in spread:
                copy.wait_recv()
            to_sibling(4 + 4 * w, plane_y, 1, 3).start()
        for w, (d, dist, plane_y) in enumerate(((1, 1, below), (-1, 3, above))):
            for k, copy in enumerate(yn[d]):
                copy.wait_recv()
                to_sibling(5 + 4 * w + k, plane_y, (0, 4)[k], 1).start()
            for copy in xf[dist]:
                copy.wait_recv()
            to_sibling(7 + 4 * w, plane_y, FAR, 3).start()

    def near_there(w):
        plane_y = (below, above)[w]
        from_sibling(4 + 4 * w, plane_y, 1, 3)
        from_sibling(5 + 4 * w, plane_y, 0, 1)
        from_sibling(6 + 4 * w, plane_y, 4, 1)
        from_sibling(7 + 4 * w, plane_y, FAR, 3)

    def far_arrive():
        for copy in zs_across + xf[2]:
            copy.wait_recv()
        to_sibling(12, across, 0, NZ).start()

    from_sibling(0, y, 1, 3)
    from_sibling(1, y, 0, 1)
    from_sibling(2, y, 4, 1)
    from_sibling(3, y, FAR, 3)
    scores_into(0, 0)
    upper = y >= 2

    def near_first():
        near_arrive()
        near_there(0)

    def two_steps(i, carry):
        pl.when((i == 1) & (y == 3))(near_first)
        scores_into(1, 2 * i + 1)
        attend(0, 2 * i)
        pl.when((i == 1) & (y < 3))(near_first)
        pl.when(i == jnp.where(upper, 2, 1))(lambda: near_there(1))
        pl.when(i == 2)(far_arrive)
        pl.when(i == jnp.where(upper, 3, 2))(lambda: from_sibling(12, across, 0, NZ))
        scores_into(0, 2 * i + 2)
        attend(1, 2 * i + 1)
        pl.when(i < 3)(lambda: decode_chunk((y + jnp.where(i == 0, 0, 2 * i + 1)) % NY))
        pl.when(i == 0)(decode_rest)
        return carry

    pairs = jnp.where(upper, 6, 4)
    lax.fori_loop(0, pairs - 1, two_steps, 0)

    loads[3].wait()

    def project(row, h, dst, at):
        rows = pl.ds(row, TOK)
        inverse = 1.0 / jnp.sum(l_ref[rows, :], -1, keepdims=True)
        mixed = (acc[rows, :] * inverse).astype(bf16)
        dst[:, at * VDIM : (at + 1) * VDIM] = jnp.dot(
            mixed, vw[:, h * VDIM : (h + 1) * VDIM], preferred_element_type=f32
        ).astype(bf16)

    home = remote(
        o_guest, out.at[:, pl.ds(GUEST_COL * VDIM, 512)], o_sems.at[0], o_sems.at[1], partner
    )
    scores_into(1, 2 * pairs - 1)
    attend(0, 2 * pairs - 2)
    for h in range(8):
        project(h * TOK, h, o_own, h)
    attend(1, 2 * pairs - 1)
    decode_chunk(across)

    @pl.when(y == 0)
    def _():
        for h in range(GUEST_COL, HEADS):
            project((h + 4) * TOK, h, o_guest, h - GUEST_COL)
        home.start()

    for h in range(8, HEADS):
        project(h * TOK, h, o_own, h)
    keep = pltpu.make_async_copy(
        o_own.at[:, pl.ds(0, GUEST_COL * VDIM)], out.at[:, pl.ds(0, GUEST_COL * VDIM)], o_sems.at[2]
    )
    keep.start()
    keep_rest = pltpu.make_async_copy(
        o_own.at[:, pl.ds(GUEST_COL * VDIM, 512)], out.at[:, pl.ds(GUEST_COL * VDIM, 512)],
        o_sems.at[3],
    )
    pl.when(y < 3)(lambda: keep_rest.start())
    dmixed = dacc[...] / jnp.sum(dl[...], -1, keepdims=True)
    for h in range(HEADS):
        col = slice(h * VDIM, (h + 1) * VDIM)
        res = jnp.dot(
            dmixed[8 * h : 8 * h + 8].astype(bf16), vw[:, col], preferred_element_type=f32
        ).astype(bf16)
        dec_out[0, :, col] = res[0:4]
        dec_out[1, :, col] = res[4:8]

    for copy in sends:
        copy.wait_send()
    for w, plane_y in enumerate((below, above)):
        to_sibling(4 + 4 * w, plane_y, 1, 3).wait_send()
        to_sibling(5 + 4 * w, plane_y, 0, 1).wait_send()
        to_sibling(6 + 4 * w, plane_y, 4, 1).wait_send()
        to_sibling(7 + 4 * w, plane_y, FAR, 3).wait_send()
    to_sibling(0, y, 1, 3).wait_send()
    to_sibling(1, y, 0, 1).wait_send()
    to_sibling(2, y, 4, 1).wait_send()
    to_sibling(3, y, FAR, 3).wait_send()
    to_sibling(12, across, 0, NZ).wait_send()
    keep.wait()
    pl.when(y < 3)(lambda: keep_rest.wait())

    @pl.when(y == 0)
    def _():
        home.wait_send()

    @pl.when(y == 3)
    def _():
        q_copy.wait_send()
        home.wait_recv()


def on_device(
    prefill_hidden, down_weight, latent_gain, key_weight, value_weight, prefill_query,
    decode_hidden, decode_query, latent_cache, place_device, place_slot, context_length,
):
    half = ROPE // 2
    freq = 10000.0 ** (-(np.arange(128) % half).astype(np.float64) / half)
    freq = jnp.asarray(freq.astype(np.float32)[None])
    vmem = pl.BlockSpec(memory_space=pltpu.VMEM)
    hbm = pl.BlockSpec(memory_space=pl.ANY)
    dma = pltpu.SemaphoreType.DMA
    return pl.pallas_call(
        kernel,
        out_shape=(
            jax.ShapeDtypeStruct((TOK, HEADS * VDIM), bf16),
            jax.ShapeDtypeStruct((2, 4, HEADS * VDIM), bf16),
        ),
        in_specs=[hbm] * 8 + [pl.BlockSpec(memory_space=pltpu.SMEM)] + [hbm] * 4,
        out_specs=(hbm, vmem),
        scratch_shapes=[
            pltpu.VMEM((TOK, 896), bf16),
            pltpu.VMEM((LAT + ROPE, 896), bf16),
            pltpu.VMEM((2, 4, 896), bf16),
            pltpu.VMEM((1, LAT), f32),
            pltpu.VMEM((1, 128), f32),
            pltpu.VMEM((1, TOK), i32),
            pltpu.VMEM((1, TOK), i32),
            pltpu.VMEM((2, 4, HEADS * 192), bf16),
            pltpu.VMEM((LAT, HEADS * NOPE), bf16),
            pltpu.VMEM((LAT, HEADS * VDIM), bf16),
            pltpu.VMEM((TOK, HEADS * 192), bf16),
            pltpu.VMEM((TOK, 4 * 192), bf16),
            pltpu.VMEM((4, LAT + ROPE, 512), bf16),
            pltpu.VMEM((TOK, ROW), f32),
            pltpu.VMEM((8, ROW), f32),
            pltpu.VMEM((NHP - 1, 16, ROW), f32),
            pltpu.VMEM((NHP - 1, 8, ROW), f32),
            pltpu.VMEM((NY, NZ, NHP, 16, ROW), bf16),
            pltpu.VMEM((NY * NZ, 8, TOK), i32),
            pltpu.VMEM((TOK, ROW), bf16),
            pltpu.VMEM((5 * TQ, ROW), bf16),
            pltpu.VMEM((TOK, ROW), bf16),
            pltpu.VMEM((5 * TQ, 128), f32),
            pltpu.VMEM((5 * TQ, 128), f32),
            pltpu.VMEM((5 * TQ, LAT), f32),
            pltpu.VMEM((TOK, 128), f32),
            pltpu.VMEM((TOK, 128), f32),
            pltpu.VMEM((TOK, LAT), f32),
            pltpu.VMEM((2, TQ, CHUNK), f32),
            pltpu.VMEM((TOK, HEADS * VDIM), bf16),
            pltpu.VMEM((TOK, 4 * VDIM), bf16),
            dma((12,)), dma((2,)), dma((7,)), dma((7,)), dma((7,)), dma((7,)),
            dma((7,)), dma((7,)), dma((3,)), dma((3,)),
            dma((3,)), dma((3,)), dma((3,)), dma((3,)), dma((4,)), dma((4,)),
            dma((12,)), dma((12,)), dma((3,)), dma((3,)), dma((4,)), dma((4,)),
            dma((3,)), dma((3,)), dma((8,)), dma((8,)), dma((13,)), dma((13,)), dma((4,)),
        ],
        compiler_params=pltpu.CompilerParams(
            collective_id=0, has_side_effects=True, vmem_limit_bytes=56 << 20
        ),
    )(
        prefill_hidden, down_weight.T, decode_hidden, latent_gain.reshape(1, LAT), freq,
        place_device.reshape(1, TOK), place_slot.reshape(1, TOK), decode_query, context_length,
        key_weight, value_weight, prefill_query, latent_cache.transpose(0, 2, 1),
    )


def solution(mesh):
    in_specs = (
        P("seq", ("head", "pool")),
        P(("head", "pool"), None),
        P(),
        P(None, ("head", "pool")),
        P(None, ("head", "pool")),
        P("seq", ("head", "pool")),
        P(None, "seq", ("head", "pool")),
        P(None, "seq", ("head", "pool")),
        P("seq", None, None),
        P("seq"),
        P("seq"),
        P("seq"),
    )
    out_specs = (P("seq", ("head", "pool")), P(None, "seq", ("head", "pool")))
    return jax.shard_map(
        on_device, mesh=mesh, in_specs=in_specs, out_specs=out_specs, check_vma=False
    )
```

```python
import functools

import jax
import jax.numpy as jnp
import numpy as np
from jax import lax
from jax.experimental import pallas as pl
from jax.experimental.pallas import tpu as pltpu
from jax.sharding import PartitionSpec as P

LAT = 512
ROPE = 64
NOPE = 128
VDIM = 128
ROW = 640
TOK = 128
HEADS = 16
NY, NZ = 4, 8
CHUNK = NZ * TOK
NHP = 8
OWN, FAR = 2, 5
TQ = 512
GUEST = 4
SCALE = (NOPE + ROPE) ** (-0.5) * 1.4426950408889634
NEG = -1e30
MESH = pl.DeviceIdType.MESH
f32, bf16, i32 = jnp.float32, jnp.bfloat16, jnp.int32
NT = (((1,), (1,)), ((), ()))

STEPS = [
    [(0, 0), (1, 0), (2, 0), (3, 0), (0, 0), (0, 1), (0, 3), (0, 2)],
    [(t, c) for c in (1, 0) for t in range(4)],
    [(t, c) for c in (2, 1, 0) for t in range(4)],
    [(t, c) for c in (3, 2, 0, 1) for t in (1, 2, 3)],
]
TILE_CODE = [sum(t << (2 * n) for n, (t, c) in enumerate(row)) for row in STEPS]
CHUNK_CODE = [sum(c << (2 * n) for n, (t, c) in enumerate(row)) for row in STEPS]


def pick(y, table):
    return jnp.where(
        y == 0, table[0], jnp.where(y == 1, table[1], jnp.where(y == 2, table[2], table[3]))
    )


def finalize(summed, gain, freq, position):
    content = summed[:, :LAT]
    meansq = jnp.mean(content * content, -1, keepdims=True)
    content = content * lax.rsqrt(meansq + 1e-06) * gain
    tail = summed[:, LAT:]
    lane = lax.broadcasted_iota(i32, tail.shape, 1)
    angle = position * freq
    cosine, sine = jnp.cos(angle), jnp.sin(angle)
    swapped = jnp.where(lane < 32, -pltpu.roll(tail, 96, 1), pltpu.roll(tail, 32, 1))
    rotated = jnp.where(lane < ROPE, tail * cosine + swapped * sine, 0.0)
    return jnp.concatenate([content, rotated], -1).astype(bf16)


def kernel(
    hidden_in, down_in, dec_hidden_in, gain_in, freq_in, dev_in, slot_in, dec_query_in, context,
    key_w, value_w, query, cache,
    out, dec_out,
    hidden, down, dec_hidden, gain, freq, place_dev, place_slot, dec_query,
    kw, vw, q_own, q_far, kept,
    part, part_d, rs, rs_d, lat, meta, fresh,
    qa, qd, m_ref, l_ref, acc, dm, dl, dacc, ks, sbuf, o_own, o_guest,
    ld_sem, q_sems, rs_s, rs_r, rd_s, rd_r, mz_s, mz_r, my_s, my_r,
    ax_s, ax_r, fz_s, fz_r, nz_s, nz_r, xf_s, xf_r, yf_s, yf_r, yn_s, yn_r, yo_s, yo_r, zs_s, zs_r,
    sb_s, sb_r, o_sems,
):
    seq = lax.axis_index("seq")
    head = lax.axis_index("head")
    pool = lax.axis_index("pool")
    y, z = seq // NZ, seq % NZ
    hp = head * 4 + pool

    def at_hp(d):
        other = (hp + d) % NHP
        return other, {"head": other // 4, "pool": other % 4}

    def at_z(d):
        return {"seq": y * NZ + (z + d + NZ) % NZ}

    def at_y(d):
        return {"seq": (y + d + NY) % NY * NZ + z}

    def at_x(d):
        return {"pool": (pool + d) % 4}

    partner = {"seq": (NY - 1 - y) * NZ + z}
    sibling = {"head": 1 - head}

    def remote(src, dst, ssem, rsem, dev):
        return pltpu.make_async_remote_copy(
            src_ref=src, dst_ref=dst, send_sem=ssem, recv_sem=rsem, device_id=dev,
            device_id_type=MESH,
        )

    first_loads = [
        pltpu.make_async_copy(src, dst, ld_sem.at[4 + i])
        for i, (src, dst) in enumerate(
            (
                (hidden_in, hidden), (down_in, down), (dec_hidden_in, dec_hidden),
                (dev_in, place_dev), (slot_in, place_slot), (gain_in, gain), (freq_in, freq),
                (dec_query_in, dec_query),
            )
        )
    ]
    loads = [
        pltpu.make_async_copy(query, q_own, ld_sem.at[0]),
        pltpu.make_async_copy(key_w, kw, ld_sem.at[1]),
        pltpu.make_async_copy(cache, kept, ld_sem.at[2]),
        pltpu.make_async_copy(value_w, vw, ld_sem.at[3]),
    ]
    for copy in first_loads + loads:
        copy.start()

    barrier = pltpu.get_barrier_semaphore()
    for d in range(1, NHP):
        pl.semaphore_signal(barrier, inc=1, device_id=at_hp(d)[1], device_id_type=MESH)
    for d in range(1, NZ):
        pl.semaphore_signal(barrier, inc=1, device_id=at_z(d), device_id_type=MESH)
    for d in range(1, NY):
        pl.semaphore_signal(barrier, inc=1, device_id=at_y(d), device_id_type=MESH)

    for copy in first_loads:
        copy.wait()
    part[:, LAT:] = jnp.zeros((TOK, ROW - LAT), f32)
    part_d[:, LAT:] = jnp.zeros((8, ROW - LAT), f32)
    part[:, : LAT + ROPE] = lax.dot_general(
        hidden[...], down[...], NT, preferred_element_type=f32
    )
    dh = jnp.concatenate([dec_hidden[0].astype(f32), dec_hidden[1].astype(f32)], 0).astype(bf16)
    part_d[:, : LAT + ROPE] = lax.dot_general(dh, down[...], NT, preferred_element_type=f32)
    mine = meta.at[pl.ds(seq, 1)]
    meta[pl.ds(seq, 1), 0:1, :] = place_dev[...].reshape(1, 1, TOK)
    meta[pl.ds(seq, 1), 1:2, :] = place_slot[...].reshape(1, 1, TOK)

    pl.semaphore_wait(barrier, NHP + NZ + NY - 3)

    sends = []

    def go(copy):
        copy.start()
        sends.append(copy)
        return copy

    rs_copies, rd_copies = [], []
    for d in range(1, NHP):
        other, dev = at_hp(d)
        rows = pl.ds(pl.multiple_of(other * 16, 16), 16)
        rs_copies.append(
            go(remote(part.at[rows], rs.at[d - 1], rs_s.at[d - 1], rs_r.at[d - 1], dev))
        )
    mz = [
        go(remote(mine, mine, mz_s.at[d - 1], mz_r.at[d - 1], at_z(d))) for d in range(1, NZ)
    ]
    q_copy = remote(
        query.at[:, pl.ds(0, 768)], q_far, q_sems.at[0], q_sems.at[1], partner
    )
    pl.when(y == 3)(lambda: q_copy.start())

    m_ref[...] = jnp.full(m_ref.shape, NEG, f32)
    l_ref[...] = jnp.zeros(l_ref.shape, f32)
    dm[...] = jnp.full(dm.shape, NEG, f32)
    dl[...] = jnp.zeros(dl.shape, f32)
    dacc[...] = jnp.zeros(dacc.shape, f32)

    def clear(i, carry):
        acc[pl.ds(pl.multiple_of(i * 256, 256), 256), :] = jnp.zeros((256, LAT), f32)
        return carry

    lax.fori_loop(0, 5 * TQ // 256, clear, 0)

    def absorb(load, dst, base, rows, heads=HEADS):
        def pair(j, carry):
            col = pl.multiple_of(j * 384, 128)
            t0, t1, t2 = load(col), load(col + 128), load(col + 256)
            lane = lax.broadcasted_iota(i32, t0.shape, 1)
            low = lane < 64
            nopes = (t0, pltpu.roll(jnp.where(low, t2, t1), 64, 1))
            ropes = (jnp.where(low, t1, 0.0), jnp.where(low, pltpu.roll(t2, 64, 1), 0.0))
            both = []
            for k in range(2):
                wcol = pl.multiple_of(j * 256 + k * 128, 128)
                absorbed = lax.dot_general(
                    nopes[k].astype(bf16), kw[:, pl.ds(wcol, 128)], NT, preferred_element_type=f32
                )
                both.append(jnp.concatenate([absorbed, ropes[k]], -1))
            at = pl.multiple_of(base + 2 * j * rows, 2 * rows)
            dst[pl.ds(at, 2 * rows), :] = jnp.concatenate(both, 0).astype(bf16)
            return carry

        lax.fori_loop(0, heads // 2, pair, 0)

    loads[0].wait()
    loads[1].wait()
    absorb(lambda c: q_own[:, pl.ds(c, 128)].astype(f32), qa, 0, TOK)
    absorb(
        lambda c: jnp.concatenate(
            [dec_query[0, :, pl.ds(c, 128)], dec_query[1, :, pl.ds(c, 128)]], 0
        ).astype(f32),
        qd, 0, 8,
    )

    loads[2].wait()
    for r in range(4):
        ks[:, 512 * r : 512 * (r + 1)] = jnp.dot(
            qd[:, :LAT], kept[r, :LAT], preferred_element_type=f32
        ) + jnp.dot(qd[:, LAT : LAT + ROPE], kept[r, LAT:], preferred_element_type=f32)

    for copy in rs_copies:
        copy.wait_recv()
    first = seq * TOK + hp * 16
    summed = part[pl.ds(pl.multiple_of(hp * 16, 16), 16), :]
    for d in range(1, NHP):
        summed = summed + rs[d - 1]
    position = (first + lax.broadcasted_iota(i32, (16, 1), 0)).astype(f32)
    lat[y, OWN, hp] = finalize(summed, gain[...], freq[...], position)

    half = pl.ds(head * 4, 4)
    own_rows = lat.at[y, OWN, hp]
    ax = [
        go(remote(own_rows, own_rows, ax_s.at[d - 1], ax_r.at[d - 1], at_x(d))) for d in (1, 2, 3)
    ]
    fz = []
    for k, d in enumerate((3, 4, 5)):
        there = lat.at[y, (OWN - d) % NZ, hp]
        fz.append(go(remote(own_rows, there, fz_s.at[k], fz_r.at[k], at_z(d))))
    for d in range(1, NHP):
        rd_copies.append(
            go(remote(part_d, rs_d.at[d - 1], rd_s.at[d - 1], rd_r.at[d - 1], at_hp(d)[1]))
        )

    for copy in ax:
        copy.wait_recv()
    own_half = lat.at[y, OWN, half]
    nz = {}
    for k, d in enumerate((1, -1, 2, -2)):
        there = lat.at[y, OWN - d, half]
        nz[d] = go(remote(own_half, there, nz_s.at[k], nz_r.at[k], at_z(d)))

    yo = {}
    for k, d in enumerate((1, -1, 2)):
        yo[d] = go(remote(own_half, own_half, yo_s.at[k], yo_r.at[k], at_y(d)))

    below, above, across = (y + 3) % NY, (y + 1) % NY, (y + 2) % NY

    def along_z(k, plane_y, d):
        there = lat.at[plane_y, OWN - d, half]
        return go(
            remote(lat.at[plane_y, OWN, half], there, zs_s.at[k], zs_r.at[k], at_z(d))
        )

    yn = {1: [], -1: []}

    def to_planes(i):
        ref = lat.at[y, i, half]
        for w, d in enumerate((1, -1)):
            k = 2 * w + i // 4
            yn[d].append(go(remote(ref, ref, yn_s.at[k], yn_r.at[k], at_y(d))))

    for copy in mz:
        copy.wait_recv()
    plane = meta.at[pl.ds(pl.multiple_of(y * NZ, NZ), NZ)]
    my = [go(remote(plane, plane, my_s.at[d - 1], my_r.at[d - 1], at_y(d))) for d in range(1, NY)]

    def over_x(dist, plane_y):
        ref = lat.at[plane_y, pl.ds(FAR, 3), hp]
        return [
            go(
                remote(
                    ref, ref, xf_s.at[3 * dist + d - 1], xf_r.at[3 * dist + d - 1], at_x(d)
                )
            )
            for d in (1, 2, 3)
        ]

    for copy in fz:
        copy.wait_recv()
    xf = {0: over_x(0, y)}
    far_rows = lat.at[y, pl.ds(FAR, 3), hp]
    yf = [go(remote(far_rows, far_rows, yf_s.at[d - 1], yf_r.at[d - 1], at_y(d))) for d in (1, 2, 3)]

    def to_sibling(k, plane_y, start, count):
        ref = lat.at[plane_y, pl.ds(start, count), half]
        return remote(ref, ref, sb_s.at[k], sb_r.at[k], sibling)

    def from_sibling(k, plane_y, start, count):
        to_sibling(k, plane_y, start, count).wait_recv()

    ctx = [context[r] for r in range(4)]
    drow = lax.broadcasted_iota(i32, (TOK, 1), 0) % 4
    dstep = lax.broadcasted_iota(i32, (TOK, 1), 0) // 4 % 2

    def decode_weights(scores, mask):
        scores = jnp.where(mask, scores * SCALE, NEG)
        m_old = dm[...]
        m_new = jnp.maximum(m_old, jnp.max(scores, -1, keepdims=True))
        alpha = jnp.exp2(m_old - m_new)
        dm[...] = m_new
        expo = jnp.where(mask, jnp.exp2(scores - m_new[:, :1]), 0.0)
        total = dl[...] * alpha
        for j in range(scores.shape[1] // 128):
            total = total + expo[:, 128 * j : 128 * (j + 1)]
        dl[...] = total
        dacc[...] = dacc[...] * alpha[:, :1]
        return expo.astype(bf16)

    def decode_update(scores, mask, contents):
        expo = decode_weights(scores, mask)
        dacc[...] = dacc[...] + jnp.dot(expo, contents, preferred_element_type=f32)

    @pl.when(y == 0)
    def _():
        q_copy.wait_recv()
        absorb(lambda c: q_far[:, pl.ds(c, 128)].astype(f32), qa, GUEST * TQ, TOK, 4)

    yo[1].wait_recv()
    zs_below = [along_z(k, below, d) for k, d in enumerate((1, -1))]
    yo[-1].wait_recv()
    zs_above = [along_z(2 + k, above, d) for k, d in enumerate((1, -1))]
    for copy in rd_copies:
        copy.wait_recv()
    summed = part_d[...]
    for d in range(1, NHP):
        summed = summed + rs_d[d - 1]
    row8 = lax.broadcasted_iota(i32, (8, 1), 0)
    length = pick(row8 % 4, ctx)
    new_rows = finalize(summed, gain[...], freq[...], (length + row8 // 4).astype(f32))
    fresh[...] = jnp.concatenate([new_rows.astype(f32), jnp.zeros((TOK - 8, ROW), f32)], 0).astype(
        bf16
    )
    key = lax.broadcasted_iota(i32, (1, TOK), 1)
    decode_update(
        lax.dot_general(qd[...], fresh[...], NT, preferred_element_type=f32),
        (key < 8) & (key % 4 == drow) & (key // 4 <= dstep),
        fresh[:, :LAT],
    )
    for d in (1, -1):
        nz[d].wait_recv()
    to_sibling(0, y, 1, 3).start()
    yo[2].wait_recv()
    zs_across = [along_z(4 + k, across, d) for k, d in enumerate((1, -1, 2, -2))]
    for copy in my:
        copy.wait_recv()
    counts = jnp.zeros((16, TOK), f32)
    for b in range(NY * NZ):
        device, slot = meta[b, 0:1, :], meta[b, 1:2, :]
        here = device == seq
        high = jnp.where(here, slot // 128, -1)
        low = slot % 128
        one = lax.broadcasted_iota(i32, (16, TOK), 0) == high
        two = lax.broadcasted_iota(i32, (TOK, TOK), 0) == low
        counts = counts + lax.dot_general(
            one.astype(f32).astype(bf16), two.astype(f32).astype(bf16), NT,
            preferred_element_type=f32,
        )
    hi = lax.broadcasted_iota(i32, (16, TOK), 0)
    place = hi % 4 * 128 + lax.broadcasted_iota(i32, (16, TOK), 1)
    live = (place < pick(hi // 4, ctx)) & (counts < 0.5)
    owner = jnp.where(live, hi // 4, -1)

    def kept_rows():
        keyrow = jnp.concatenate([owner[j : j + 1, :] for j in range(16)], 1)
        expo = decode_weights(ks[...], keyrow == drow)
        mixed = dacc[...]
        for r in range(4):
            mixed = mixed + lax.dot_general(
                expo[:, 512 * r : 512 * (r + 1)], kept[r, :LAT], NT, preferred_element_type=f32
            )
        dacc[...] = mixed

    for d in (2, -2):
        nz[d].wait_recv()
        to_planes(OWN - d)
    to_sibling(1, y, 0, 1).start()
    to_sibling(2, y, 4, 1).start()
    for copy in xf[0]:
        copy.wait_recv()
    to_sibling(3, y, FAR, 3).start()
    for d in (1, 3, 2):
        yf[d - 1].wait_recv()
        xf[d] = over_x(d, (y - d + NY) % NY)

    kept_rows()

    def decode_chunk(c):
        pieces = []
        for j in range(NZ):
            tile = meta[pl.ds(c * NZ + (z + j + 6) % NZ, 1), :, :][0]
            pieces.append(jnp.where(tile[0:1] == seq, tile[1:2] // 512, -1))
        keyrow = jnp.concatenate(pieces, 1)
        scores = lax.dot_general(
            qd[...], lat[c].reshape(CHUNK, ROW), NT, preferred_element_type=f32
        )
        decode_update(scores, keyrow == drow, lat[c, :, :, :, :LAT].reshape(CHUNK, LAT))

    tile_code, chunk_code = pick(y, TILE_CODE), pick(y, CHUNK_CODE)

    def step_of(n):
        tile = jnp.where((y == 0) & (n >= 4), GUEST, (tile_code >> (2 * n)) & 3)
        return tile, (chunk_code >> (2 * n)) & 3

    def rows_of(tile):
        return pl.ds(pl.multiple_of(tile * TQ, TQ), TQ)

    def scores_into(slot, n):
        tile, c = step_of(n)
        sbuf[slot] = lax.dot_general(
            qa[rows_of(tile), :], lat[c].reshape(CHUNK, ROW), NT, preferred_element_type=f32
        )

    def attend(slot, n):
        tile, c = step_of(n)
        rows = rows_of(tile)
        limit = jnp.where(tile == GUEST, 3, y)
        start = jnp.where(c == limit, z * TOK, 1 << 20)
        token = start + lax.broadcasted_iota(i32, (TQ, 1), 0) % TOK
        key = (lax.broadcasted_iota(i32, (1, CHUNK), 1) + (z + 6) * TOK) & (CHUNK - 1)
        allowed = key <= token
        scores = jnp.where(allowed, sbuf[slot], NEG)
        m_old = m_ref[rows, :]
        m_new = jnp.maximum(m_old, jnp.max(scores, -1, keepdims=True) * SCALE)
        alpha = jnp.exp2(m_old - m_new)
        m_ref[rows, :] = m_new
        expo = jnp.exp2(scores * SCALE - m_new[:, :1])
        total = l_ref[rows, :] * alpha
        for j in range(CHUNK // 128):
            total = total + expo[:, 128 * j : 128 * (j + 1)]
        l_ref[rows, :] = total
        acc[rows, :] = acc[rows, :] * alpha[:, :1] + jnp.dot(
            expo.astype(bf16), lat[c, :, :, :, :LAT].reshape(CHUNK, LAT), preferred_element_type=f32
        )

    def near_arrive():
        for w, (plane_y, spread) in enumerate(((below, zs_below), (above, zs_above))):
            for copy in spread:
                copy.wait_recv()
            to_sibling(4 + 4 * w, plane_y, 1, 3).start()
        for w, (d, dist, plane_y) in enumerate(((1, 1, below), (-1, 3, above))):
            for k, copy in enumerate(yn[d]):
                copy.wait_recv()
                to_sibling(5 + 4 * w + k, plane_y, (0, 4)[k], 1).start()
            for copy in xf[dist]:
                copy.wait_recv()
            to_sibling(7 + 4 * w, plane_y, FAR, 3).start()

    def near_there(w):
        plane_y = (below, above)[w]
        from_sibling(4 + 4 * w, plane_y, 1, 3)
        from_sibling(5 + 4 * w, plane_y, 0, 1)
        from_sibling(6 + 4 * w, plane_y, 4, 1)
        from_sibling(7 + 4 * w, plane_y, FAR, 3)

    def far_arrive():
        for copy in zs_across + xf[2]:
            copy.wait_recv()
        to_sibling(12, across, 0, NZ).start()

    from_sibling(0, y, 1, 3)
    from_sibling(1, y, 0, 1)
    from_sibling(2, y, 4, 1)
    from_sibling(3, y, FAR, 3)
    scores_into(0, 0)
    upper = y >= 2

    def near_first():
        near_arrive()
        near_there(0)

    def two_steps(i, carry):
        pl.when((i == 1) & (y == 3))(near_first)
        scores_into(1, 2 * i + 1)
        attend(0, 2 * i)
        pl.when((i == 1) & (y < 3))(near_first)
        pl.when(i == jnp.where(upper, 2, 1))(lambda: near_there(1))
        pl.when(i == 2)(far_arrive)
        pl.when(i == jnp.where(upper, 3, 2))(lambda: from_sibling(12, across, 0, NZ))
        scores_into(0, 2 * i + 2)
        attend(1, 2 * i + 1)
        pl.when(i < 3)(lambda: decode_chunk((y + jnp.where(i == 0, 0, 2 * i + 1)) % NY))
        pl.when(i == jnp.where(upper, 3, 2))(lambda: decode_chunk(across))
        return carry

    pairs = jnp.where(upper, 6, 4)
    lax.fori_loop(0, pairs - 1, two_steps, 0)

    loads[3].wait()

    dmixed = dacc[...] * (1.0 / jnp.sum(dl[...], -1, keepdims=True))

    def mixed_of(row):
        rows = pl.ds(row, TOK)
        return acc[rows, :] * (1.0 / jnp.sum(l_ref[rows, :], -1, keepdims=True))

    def through(mixed, h):
        weight = vw[:, h * VDIM : (h + 1) * VDIM]
        return jnp.dot(mixed.astype(bf16), weight, preferred_element_type=f32).astype(bf16)

    def project(h):
        both = jnp.concatenate([mixed_of(h * TOK), dmixed[8 * h : 8 * h + 8]], 0)
        res = through(both, h)
        col = slice(h * VDIM, (h + 1) * VDIM)
        o_own[:, col] = res[:TOK]
        dec_out[0, :, col] = res[TOK : TOK + 4]
        dec_out[1, :, col] = res[TOK + 4 :]

    home = remote(o_guest, out.at[:, pl.ds(0, 512)], o_sems.at[0], o_sems.at[1], partner)

    def keep(k):
        cols = pl.ds(512 * k, 512)
        return pltpu.make_async_copy(o_own.at[:, cols], out.at[:, cols], o_sems.at[2 + k])

    scores_into(1, 2 * pairs - 1)
    attend(0, 2 * pairs - 2)
    for h in range(12):
        project(h)
    attend(1, 2 * pairs - 1)
    pl.when(y < 3)(lambda: keep(0).start())
    keep(1).start()
    keep(2).start()

    @pl.when(y == 0)
    def _():
        for h in range(4):
            o_guest[:, h * VDIM : (h + 1) * VDIM] = through(mixed_of(GUEST * TQ + h * TOK), h)
        home.start()

    for h in range(12, HEADS):
        project(h)
    keep(3).start()
    for copy in sends:
        copy.wait_send()
    for w, plane_y in enumerate((below, above)):
        to_sibling(4 + 4 * w, plane_y, 1, 3).wait_send()
        to_sibling(5 + 4 * w, plane_y, 0, 1).wait_send()
        to_sibling(6 + 4 * w, plane_y, 4, 1).wait_send()
        to_sibling(7 + 4 * w, plane_y, FAR, 3).wait_send()
    to_sibling(0, y, 1, 3).wait_send()
    to_sibling(1, y, 0, 1).wait_send()
    to_sibling(2, y, 4, 1).wait_send()
    to_sibling(3, y, FAR, 3).wait_send()
    to_sibling(12, across, 0, NZ).wait_send()
    pl.when(y < 3)(lambda: keep(0).wait())
    for k in (1, 2, 3):
        keep(k).wait()

    @pl.when(y == 0)
    def _():
        home.wait_send()

    @pl.when(y == 3)
    def _():
        q_copy.wait_send()
        home.wait_recv()


def hand_over(a, b, a_out, b_out):
    a_out[...] = a[...]
    b_out[...] = b[...]


def on_device(
    prefill_hidden, down_weight, latent_gain, key_weight, value_weight, prefill_query,
    decode_hidden, decode_query, latent_cache, place_device, place_slot, context_length,
):
    half = ROPE // 2
    freq = 10000.0 ** (-(np.arange(128) % half).astype(np.float64) / half)
    freq = jnp.asarray(freq.astype(np.float32)[None])
    vmem = pl.BlockSpec(memory_space=pltpu.VMEM)
    hbm = pl.BlockSpec(memory_space=pl.ANY)
    dma = pltpu.SemaphoreType.DMA
    out, dec_out = pl.pallas_call(
        kernel,
        out_shape=(
            jax.ShapeDtypeStruct((TOK, HEADS * VDIM), bf16),
            jax.ShapeDtypeStruct((2, 4, HEADS * VDIM), bf16),
        ),
        in_specs=[hbm] * 8 + [pl.BlockSpec(memory_space=pltpu.SMEM)] + [hbm] * 4,
        out_specs=(hbm, vmem),
        scratch_shapes=[
            pltpu.VMEM((TOK, 896), bf16),
            pltpu.VMEM((LAT + ROPE, 896), bf16),
            pltpu.VMEM((2, 4, 896), bf16),
            pltpu.VMEM((1, LAT), f32),
            pltpu.VMEM((1, 128), f32),
            pltpu.VMEM((1, TOK), i32),
            pltpu.VMEM((1, TOK), i32),
            pltpu.VMEM((2, 4, HEADS * 192), bf16),
            pltpu.VMEM((LAT, HEADS * NOPE), bf16),
            pltpu.VMEM((LAT, HEADS * VDIM), bf16),
            pltpu.VMEM((TOK, HEADS * 192), bf16),
            pltpu.VMEM((TOK, 4 * 192), bf16),
            pltpu.VMEM((4, LAT + ROPE, 512), bf16),
            pltpu.VMEM((TOK, ROW), f32),
            pltpu.VMEM((8, ROW), f32),
            pltpu.VMEM((NHP - 1, 16, ROW), f32),
            pltpu.VMEM((NHP - 1, 8, ROW), f32),
            pltpu.VMEM((NY, NZ, NHP, 16, ROW), bf16),
            pltpu.VMEM((NY * NZ, 8, TOK), i32),
            pltpu.VMEM((TOK, ROW), bf16),
            pltpu.VMEM((5 * TQ, ROW), bf16),
            pltpu.VMEM((TOK, ROW), bf16),
            pltpu.VMEM((5 * TQ, 128), f32),
            pltpu.VMEM((5 * TQ, 128), f32),
            pltpu.VMEM((5 * TQ, LAT), f32),
            pltpu.VMEM((TOK, 128), f32),
            pltpu.VMEM((TOK, 128), f32),
            pltpu.VMEM((TOK, LAT), f32),
            pltpu.VMEM((TOK, 2048), f32),
            pltpu.VMEM((2, TQ, CHUNK), f32),
            pltpu.VMEM((TOK, HEADS * VDIM), bf16),
            pltpu.VMEM((TOK, 4 * VDIM), bf16),
            dma((12,)), dma((2,)), dma((7,)), dma((7,)), dma((7,)), dma((7,)),
            dma((7,)), dma((7,)), dma((3,)), dma((3,)),
            dma((3,)), dma((3,)), dma((3,)), dma((3,)), dma((4,)), dma((4,)),
            dma((12,)), dma((12,)), dma((3,)), dma((3,)), dma((4,)), dma((4,)),
            dma((3,)), dma((3,)), dma((8,)), dma((8,)), dma((13,)), dma((13,)), dma((6,)),
        ],
        compiler_params=pltpu.CompilerParams(
            collective_id=0, has_side_effects=True, vmem_limit_bytes=56 << 20
        ),
    )(
        prefill_hidden, down_weight.T, decode_hidden, latent_gain.reshape(1, LAT), freq,
        place_device.reshape(1, TOK), place_slot.reshape(1, TOK), decode_query, context_length,
        key_weight, value_weight, prefill_query, latent_cache.transpose(0, 2, 1),
    )
    return pl.pallas_call(
        hand_over,
        out_shape=(
            jax.ShapeDtypeStruct((TOK, HEADS * VDIM), bf16),
            jax.ShapeDtypeStruct((2, 4, HEADS * VDIM), bf16),
        ),
        in_specs=[vmem, vmem],
        out_specs=(vmem, vmem),
    )(out, dec_out)


def solution(mesh):
    in_specs = (
        P("seq", ("head", "pool")),
        P(("head", "pool"), None),
        P(),
        P(None, ("head", "pool")),
        P(None, ("head", "pool")),
        P("seq", ("head", "pool")),
        P(None, "seq", ("head", "pool")),
        P(None, "seq", ("head", "pool")),
        P("seq", None, None),
        P("seq"),
        P("seq"),
        P("seq"),
    )
    out_specs = (P("seq", ("head", "pool")), P(None, "seq", ("head", "pool")))
    return jax.shard_map(
        on_device, mesh=mesh, in_specs=in_specs, out_specs=out_specs, check_vma=False
    )
```

```python
import functools

import jax
import jax.numpy as jnp
import numpy as np
from jax import lax
from jax.experimental import pallas as pl
from jax.experimental.pallas import tpu as pltpu
from jax.sharding import PartitionSpec as P

LAT = 512
ROPE = 64
NOPE = 128
VDIM = 128
ROW = 640
TOK = 128
HEADS = 16
NY, NZ = 4, 8
CHUNK = NZ * TOK
NHP = 8
OWN, FAR = 2, 5
TQ = 512
GUEST = 4
SCALE = (NOPE + ROPE) ** (-0.5) * 1.4426950408889634
NEG = -1e30
MESH = pl.DeviceIdType.MESH
f32, bf16, i32 = jnp.float32, jnp.bfloat16, jnp.int32
NT = (((1,), (1,)), ((), ()))

STEPS = [
    [(0, 0), (1, 0), (2, 0), (3, 0), (0, 0), (0, 1), (0, 3), (0, 2)],
    [(t, c) for c in (1, 0) for t in range(4)],
    [(t, c) for c in (2, 1, 0) for t in range(4)],
    [(t, c) for c in (3, 2, 0, 1) for t in (1, 2, 3)],
]
TILE_CODE = [sum(t << (2 * n) for n, (t, c) in enumerate(row)) for row in STEPS]
CHUNK_CODE = [sum(c << (2 * n) for n, (t, c) in enumerate(row)) for row in STEPS]


def pick(y, table):
    return jnp.where(
        y == 0, table[0], jnp.where(y == 1, table[1], jnp.where(y == 2, table[2], table[3]))
    )


def finalize(summed, gain, freq, position):
    content = summed[:, :LAT]
    meansq = jnp.mean(content * content, -1, keepdims=True)
    content = content * lax.rsqrt(meansq + 1e-06) * gain
    tail = summed[:, LAT:]
    lane = lax.broadcasted_iota(i32, tail.shape, 1)
    angle = position * freq
    cosine, sine = jnp.cos(angle), jnp.sin(angle)
    swapped = jnp.where(lane < 32, -pltpu.roll(tail, 96, 1), pltpu.roll(tail, 32, 1))
    rotated = jnp.where(lane < ROPE, tail * cosine + swapped * sine, 0.0)
    return jnp.concatenate([content, rotated], -1).astype(bf16)


def kernel(
    hidden_in, down_in, dec_hidden_in, gain_in, freq_in, dev_in, slot_in, dec_query_in, context,
    key_w, value_w, query, cache,
    out, dec_out,
    hidden, down, dec_hidden, gain, freq, place_dev, place_slot, dec_query,
    kw, vw, q_own, q_far, kept,
    part, part_d, rs, rs_d, lat, meta, fresh,
    qa, qd, m_ref, l_ref, acc, dm, dl, dacc, ks, sbuf, o_own, o_guest,
    ld_sem, q_sems, rs_s, rs_r, rd_s, rd_r, mz_s, mz_r, my_s, my_r,
    ax_s, ax_r, fz_s, fz_r, nz_s, nz_r, xf_s, xf_r, yf_s, yf_r, yn_s, yn_r, yo_s, yo_r, zs_s, zs_r,
    sb_s, sb_r, o_sems,
):
    seq = lax.axis_index("seq")
    head = lax.axis_index("head")
    pool = lax.axis_index("pool")
    y, z = seq // NZ, seq % NZ
    hp = head * 4 + pool

    def at_hp(d):
        other = (hp + d) % NHP
        return other, {"head": other // 4, "pool": other % 4}

    def at_z(d):
        return {"seq": y * NZ + (z + d + NZ) % NZ}

    def at_y(d):
        return {"seq": (y + d + NY) % NY * NZ + z}

    def at_x(d):
        return {"pool": (pool + d) % 4}

    partner = {"seq": (NY - 1 - y) * NZ + z}
    sibling = {"head": 1 - head}

    def remote(src, dst, ssem, rsem, dev):
        return pltpu.make_async_remote_copy(
            src_ref=src, dst_ref=dst, send_sem=ssem, recv_sem=rsem, device_id=dev,
            device_id_type=MESH,
        )

    first_loads = [
        pltpu.make_async_copy(src, dst, ld_sem.at[4 + i])
        for i, (src, dst) in enumerate(
            (
                (hidden_in, hidden), (down_in, down), (dec_hidden_in, dec_hidden),
                (dev_in, place_dev), (slot_in, place_slot), (gain_in, gain), (freq_in, freq),
                (dec_query_in, dec_query),
            )
        )
    ]
    loads = [
        pltpu.make_async_copy(query, q_own, ld_sem.at[0]),
        pltpu.make_async_copy(key_w, kw, ld_sem.at[1]),
        pltpu.make_async_copy(cache, kept, ld_sem.at[2]),
        pltpu.make_async_copy(value_w, vw, ld_sem.at[3]),
    ]
    for copy in first_loads + loads:
        copy.start()

    barrier = pltpu.get_barrier_semaphore()
    for d in range(1, NHP):
        pl.semaphore_signal(barrier, inc=1, device_id=at_hp(d)[1], device_id_type=MESH)
    for d in range(1, NZ):
        pl.semaphore_signal(barrier, inc=1, device_id=at_z(d), device_id_type=MESH)
    for d in range(1, NY):
        pl.semaphore_signal(barrier, inc=1, device_id=at_y(d), device_id_type=MESH)

    for copy in first_loads:
        copy.wait()
    part[:, LAT:] = jnp.zeros((TOK, ROW - LAT), f32)
    part_d[:, LAT:] = jnp.zeros((8, ROW - LAT), f32)
    part[:, : LAT + ROPE] = lax.dot_general(
        hidden[...], down[...], NT, preferred_element_type=f32
    )
    dh = jnp.concatenate([dec_hidden[0].astype(f32), dec_hidden[1].astype(f32)], 0).astype(bf16)
    part_d[:, : LAT + ROPE] = lax.dot_general(dh, down[...], NT, preferred_element_type=f32)
    mine = meta.at[pl.ds(seq, 1)]
    meta[pl.ds(seq, 1), 0:1, :] = place_dev[...].reshape(1, 1, TOK)
    meta[pl.ds(seq, 1), 1:2, :] = place_slot[...].reshape(1, 1, TOK)

    pl.semaphore_wait(barrier, NHP + NZ + NY - 3)

    sends = []

    def go(copy):
        copy.start()
        sends.append(copy)
        return copy

    rs_copies, rd_copies = [], []
    for d in range(1, NHP):
        other, dev = at_hp(d)
        rows = pl.ds(pl.multiple_of(other * 16, 16), 16)
        rs_copies.append(
            go(remote(part.at[rows], rs.at[d - 1], rs_s.at[d - 1], rs_r.at[d - 1], dev))
        )
    mz = [
        go(remote(mine, mine, mz_s.at[d - 1], mz_r.at[d - 1], at_z(d))) for d in range(1, NZ)
    ]
    q_copy = remote(
        query.at[:, pl.ds(0, 768)], q_far, q_sems.at[0], q_sems.at[1], partner
    )
    pl.when(y == 3)(lambda: q_copy.start())

    m_ref[...] = jnp.full(m_ref.shape, NEG, f32)
    l_ref[...] = jnp.zeros(l_ref.shape, f32)
    dm[...] = jnp.full(dm.shape, NEG, f32)
    dl[...] = jnp.zeros(dl.shape, f32)
    dacc[...] = jnp.zeros(dacc.shape, f32)

    def clear(i, carry):
        acc[pl.ds(pl.multiple_of(i * 256, 256), 256), :] = jnp.zeros((256, LAT), f32)
        return carry

    lax.fori_loop(0, 5 * TQ // 256, clear, 0)

    def absorb(load, dst, base, rows, heads=HEADS):
        def pair(j, carry):
            col = pl.multiple_of(j * 384, 128)
            t0, t1, t2 = load(col), load(col + 128), load(col + 256)
            lane = lax.broadcasted_iota(i32, t0.shape, 1)
            low = lane < 64
            nopes = (t0, pltpu.roll(jnp.where(low, t2, t1), 64, 1))
            ropes = (jnp.where(low, t1, 0.0), jnp.where(low, pltpu.roll(t2, 64, 1), 0.0))
            both = []
            for k in range(2):
                wcol = pl.multiple_of(j * 256 + k * 128, 128)
                absorbed = lax.dot_general(
                    nopes[k].astype(bf16), kw[:, pl.ds(wcol, 128)], NT, preferred_element_type=f32
                )
                both.append(jnp.concatenate([absorbed, ropes[k]], -1))
            at = pl.multiple_of(base + 2 * j * rows, 2 * rows)
            dst[pl.ds(at, 2 * rows), :] = jnp.concatenate(both, 0).astype(bf16)
            return carry

        lax.fori_loop(0, heads // 2, pair, 0)

    loads[0].wait()
    loads[1].wait()
    absorb(lambda c: q_own[:, pl.ds(c, 128)].astype(f32), qa, 0, TOK)
    absorb(
        lambda c: jnp.concatenate(
            [dec_query[0, :, pl.ds(c, 128)], dec_query[1, :, pl.ds(c, 128)]], 0
        ).astype(f32),
        qd, 0, 8,
    )

    loads[2].wait()
    for r in range(4):
        ks[:, 512 * r : 512 * (r + 1)] = jnp.dot(
            qd[:, :LAT], kept[r, :LAT], preferred_element_type=f32
        ) + jnp.dot(qd[:, LAT : LAT + ROPE], kept[r, LAT:], preferred_element_type=f32)

    for copy in rs_copies:
        copy.wait_recv()
    first = seq * TOK + hp * 16
    summed = part[pl.ds(pl.multiple_of(hp * 16, 16), 16), :]
    for d in range(1, NHP):
        summed = summed + rs[d - 1]
    position = (first + lax.broadcasted_iota(i32, (16, 1), 0)).astype(f32)
    lat[y, OWN, hp] = finalize(summed, gain[...], freq[...], position)

    half = pl.ds(head * 4, 4)
    own_rows = lat.at[y, OWN, hp]
    ax = [
        go(remote(own_rows, own_rows, ax_s.at[d - 1], ax_r.at[d - 1], at_x(d))) for d in (1, 2, 3)
    ]
    fz = []
    for k, d in enumerate((3, 4, 5)):
        there = lat.at[y, (OWN - d) % NZ, hp]
        fz.append(go(remote(own_rows, there, fz_s.at[k], fz_r.at[k], at_z(d))))
    for d in range(1, NHP):
        rd_copies.append(
            go(remote(part_d, rs_d.at[d - 1], rd_s.at[d - 1], rd_r.at[d - 1], at_hp(d)[1]))
        )

    for copy in ax:
        copy.wait_recv()
    own_half = lat.at[y, OWN, half]
    nz = {}
    for k, d in enumerate((1, -1, 2, -2)):
        there = lat.at[y, OWN - d, half]
        nz[d] = go(remote(own_half, there, nz_s.at[k], nz_r.at[k], at_z(d)))

    yo = {}
    for k, d in enumerate((1, -1, 2)):
        yo[d] = go(remote(own_half, own_half, yo_s.at[k], yo_r.at[k], at_y(d)))

    below, above, across = (y + 3) % NY, (y + 1) % NY, (y + 2) % NY

    def along_z(k, plane_y, d):
        there = lat.at[plane_y, OWN - d, half]
        return go(
            remote(lat.at[plane_y, OWN, half], there, zs_s.at[k], zs_r.at[k], at_z(d))
        )

    yn = {1: [], -1: []}

    def to_planes(i):
        ref = lat.at[y, i, half]
        for w, d in enumerate((1, -1)):
            k = 2 * w + i // 4
            yn[d].append(go(remote(ref, ref, yn_s.at[k], yn_r.at[k], at_y(d))))

    for copy in mz:
        copy.wait_recv()
    plane = meta.at[pl.ds(pl.multiple_of(y * NZ, NZ), NZ)]
    my = [go(remote(plane, plane, my_s.at[d - 1], my_r.at[d - 1], at_y(d))) for d in range(1, NY)]

    def over_x(dist, plane_y):
        ref = lat.at[plane_y, pl.ds(FAR, 3), hp]
        return [
            go(
                remote(
                    ref, ref, xf_s.at[3 * dist + d - 1], xf_r.at[3 * dist + d - 1], at_x(d)
                )
            )
            for d in (1, 2, 3)
        ]

    for copy in fz:
        copy.wait_recv()
    xf = {0: over_x(0, y)}
    far_rows = lat.at[y, pl.ds(FAR, 3), hp]
    yf = [go(remote(far_rows, far_rows, yf_s.at[d - 1], yf_r.at[d - 1], at_y(d))) for d in (1, 2, 3)]

    def to_sibling(k, plane_y, start, count):
        ref = lat.at[plane_y, pl.ds(start, count), half]
        return remote(ref, ref, sb_s.at[k], sb_r.at[k], sibling)

    def from_sibling(k, plane_y, start, count):
        to_sibling(k, plane_y, start, count).wait_recv()

    ctx = [context[r] for r in range(4)]
    drow = lax.broadcasted_iota(i32, (TOK, 1), 0) % 4
    dstep = lax.broadcasted_iota(i32, (TOK, 1), 0) // 4 % 2

    def decode_weights(scores, mask):
        scores = jnp.where(mask, scores * SCALE, NEG)
        m_old = dm[...]
        m_new = jnp.maximum(m_old, jnp.max(scores, -1, keepdims=True))
        alpha = jnp.exp2(m_old - m_new)
        dm[...] = m_new
        expo = jnp.where(mask, jnp.exp2(scores - m_new[:, :1]), 0.0)
        total = dl[...] * alpha
        for j in range(scores.shape[1] // 128):
            total = total + expo[:, 128 * j : 128 * (j + 1)]
        dl[...] = total
        dacc[...] = dacc[...] * alpha[:, :1]
        return expo.astype(bf16)

    def decode_update(scores, mask, contents):
        expo = decode_weights(scores, mask)
        dacc[...] = dacc[...] + jnp.dot(expo, contents, preferred_element_type=f32)

    @pl.when(y == 0)
    def _():
        q_copy.wait_recv()
        absorb(lambda c: q_far[:, pl.ds(c, 128)].astype(f32), qa, GUEST * TQ, TOK, 4)

    yo[1].wait_recv()
    zs_below = [along_z(k, below, d) for k, d in enumerate((1, -1))]
    yo[-1].wait_recv()
    zs_above = [along_z(2 + k, above, d) for k, d in enumerate((1, -1))]
    for copy in rd_copies:
        copy.wait_recv()
    summed = part_d[...]
    for d in range(1, NHP):
        summed = summed + rs_d[d - 1]
    row8 = lax.broadcasted_iota(i32, (8, 1), 0)
    length = pick(row8 % 4, ctx)
    new_rows = finalize(summed, gain[...], freq[...], (length + row8 // 4).astype(f32))
    fresh[...] = jnp.concatenate([new_rows.astype(f32), jnp.zeros((TOK - 8, ROW), f32)], 0).astype(
        bf16
    )
    key = lax.broadcasted_iota(i32, (1, TOK), 1)
    decode_update(
        lax.dot_general(qd[...], fresh[...], NT, preferred_element_type=f32),
        (key < 8) & (key % 4 == drow) & (key // 4 <= dstep),
        fresh[:, :LAT],
    )
    for d in (1, -1):
        nz[d].wait_recv()
    to_sibling(0, y, 1, 3).start()
    yo[2].wait_recv()
    zs_across = [along_z(4 + k, across, d) for k, d in enumerate((1, -1, 2, -2))]
    for copy in my:
        copy.wait_recv()
    counts = jnp.zeros((16, TOK), f32)
    for b in range(NY * NZ):
        device, slot = meta[b, 0:1, :], meta[b, 1:2, :]
        here = device == seq
        high = jnp.where(here, slot // 128, -1)
        low = slot % 128
        one = lax.broadcasted_iota(i32, (16, TOK), 0) == high
        two = lax.broadcasted_iota(i32, (TOK, TOK), 0) == low
        counts = counts + lax.dot_general(
            one.astype(f32).astype(bf16), two.astype(f32).astype(bf16), NT,
            preferred_element_type=f32,
        )
    hi = lax.broadcasted_iota(i32, (16, TOK), 0)
    place = hi % 4 * 128 + lax.broadcasted_iota(i32, (16, TOK), 1)
    live = (place < pick(hi // 4, ctx)) & (counts < 0.5)
    owner = jnp.where(live, hi // 4, -1)

    def kept_rows():
        keyrow = jnp.concatenate([owner[j : j + 1, :] for j in range(16)], 1)
        expo = decode_weights(ks[...], keyrow == drow)
        mixed = dacc[...]
        for r in range(4):
            mixed = mixed + lax.dot_general(
                expo[:, 512 * r : 512 * (r + 1)], kept[r, :LAT], NT, preferred_element_type=f32
            )
        dacc[...] = mixed

    for d in (2, -2):
        nz[d].wait_recv()
        to_planes(OWN - d)
    to_sibling(1, y, 0, 1).start()
    to_sibling(2, y, 4, 1).start()
    for copy in xf[0]:
        copy.wait_recv()
    to_sibling(3, y, FAR, 3).start()
    for d in (1, 3, 2):
        yf[d - 1].wait_recv()
        xf[d] = over_x(d, (y - d + NY) % NY)

    kept_rows()

    def decode_chunks(*planes):
        pieces, scores = [], []
        for c in planes:
            for j in range(NZ):
                tile = meta[pl.ds(c * NZ + (z + j + 6) % NZ, 1), :, :][0]
                pieces.append(jnp.where(tile[0:1] == seq, tile[1:2] // 512, -1))
            scores.append(
                lax.dot_general(
                    qd[...], lat[c].reshape(CHUNK, ROW), NT, preferred_element_type=f32
                )
            )
        expo = decode_weights(jnp.concatenate(scores, 1), jnp.concatenate(pieces, 1) == drow)
        mixed = dacc[...]
        for k, c in enumerate(planes):
            mixed = mixed + jnp.dot(
                expo[:, CHUNK * k : CHUNK * (k + 1)], lat[c, :, :, :, :LAT].reshape(CHUNK, LAT),
                preferred_element_type=f32,
            )
        dacc[...] = mixed

    tile_code, chunk_code = pick(y, TILE_CODE), pick(y, CHUNK_CODE)

    def step_of(n):
        tile = jnp.where((y == 0) & (n >= 4), GUEST, (tile_code >> (2 * n)) & 3)
        return tile, (chunk_code >> (2 * n)) & 3

    def rows_of(tile):
        return pl.ds(pl.multiple_of(tile * TQ, TQ), TQ)

    def scores_into(slot, n):
        tile, c = step_of(n)
        sbuf[slot] = lax.dot_general(
            qa[rows_of(tile), :], lat[c].reshape(CHUNK, ROW), NT, preferred_element_type=f32
        )

    def attend(slot, n):
        tile, c = step_of(n)
        rows = rows_of(tile)
        limit = jnp.where(tile == GUEST, 3, y)
        start = jnp.where(c == limit, z * TOK, 1 << 20)
        token = start + lax.broadcasted_iota(i32, (TQ, 1), 0) % TOK
        key = (lax.broadcasted_iota(i32, (1, CHUNK), 1) + (z + 6) * TOK) & (CHUNK - 1)
        allowed = key <= token
        scores = jnp.where(allowed, sbuf[slot], NEG)
        m_old = m_ref[rows, :]
        m_new = jnp.maximum(m_old, jnp.max(scores, -1, keepdims=True) * SCALE)
        alpha = jnp.exp2(m_old - m_new)
        m_ref[rows, :] = m_new
        expo = jnp.exp2(scores * SCALE - m_new[:, :1])
        total = l_ref[rows, :] * alpha
        for j in range(CHUNK // 128):
            total = total + expo[:, 128 * j : 128 * (j + 1)]
        l_ref[rows, :] = total
        acc[rows, :] = acc[rows, :] * alpha[:, :1] + jnp.dot(
            expo.astype(bf16), lat[c, :, :, :, :LAT].reshape(CHUNK, LAT), preferred_element_type=f32
        )

    def near_arrive():
        for w, (plane_y, spread) in enumerate(((below, zs_below), (above, zs_above))):
            for copy in spread:
                copy.wait_recv()
            to_sibling(4 + 4 * w, plane_y, 1, 3).start()
        for w, (d, dist, plane_y) in enumerate(((1, 1, below), (-1, 3, above))):
            for k, copy in enumerate(yn[d]):
                copy.wait_recv()
                to_sibling(5 + 4 * w + k, plane_y, (0, 4)[k], 1).start()
            for copy in xf[dist]:
                copy.wait_recv()
            to_sibling(7 + 4 * w, plane_y, FAR, 3).start()

    def near_there(w):
        plane_y = (below, above)[w]
        from_sibling(4 + 4 * w, plane_y, 1, 3)
        from_sibling(5 + 4 * w, plane_y, 0, 1)
        from_sibling(6 + 4 * w, plane_y, 4, 1)
        from_sibling(7 + 4 * w, plane_y, FAR, 3)

    def far_arrive():
        for copy in zs_across + xf[2]:
            copy.wait_recv()
        to_sibling(12, across, 0, NZ).start()

    from_sibling(0, y, 1, 3)
    from_sibling(1, y, 0, 1)
    from_sibling(2, y, 4, 1)
    from_sibling(3, y, FAR, 3)
    scores_into(0, 0)
    upper = y >= 2

    def near_first():
        near_arrive()
        near_there(0)

    def two_steps(i, carry):
        pl.when((i == 1) & (y == 3))(near_first)
        scores_into(1, 2 * i + 1)
        attend(0, 2 * i)
        pl.when((i == 1) & (y < 3))(near_first)
        pl.when(i == jnp.where(upper, 2, 1))(lambda: near_there(1))
        pl.when(i == 2)(far_arrive)
        pl.when(i == jnp.where(upper, 3, 2))(lambda: from_sibling(12, across, 0, NZ))
        scores_into(0, 2 * i + 2)
        attend(1, 2 * i + 1)
        pl.when(i == jnp.where(upper, 3, 2))(lambda: decode_chunks(y, below, above, across))
        return carry

    pairs = jnp.where(upper, 6, 4)
    lax.fori_loop(0, pairs - 1, two_steps, 0)

    loads[3].wait()

    dmixed = dacc[...] * (1.0 / jnp.sum(dl[...], -1, keepdims=True))

    def mixed_of(row):
        rows = pl.ds(row, TOK)
        return acc[rows, :] * (1.0 / jnp.sum(l_ref[rows, :], -1, keepdims=True))

    def through(mixed, h):
        weight = vw[:, h * VDIM : (h + 1) * VDIM]
        return jnp.dot(mixed.astype(bf16), weight, preferred_element_type=f32).astype(bf16)

    def project(h):
        both = jnp.concatenate([mixed_of(h * TOK), dmixed[8 * h : 8 * h + 8]], 0)
        res = through(both, h)
        col = slice(h * VDIM, (h + 1) * VDIM)
        o_own[:, col] = res[:TOK]
        dec_out[0, :, col] = res[TOK : TOK + 4]
        dec_out[1, :, col] = res[TOK + 4 :]

    home = remote(o_guest, out.at[:, pl.ds(0, 512)], o_sems.at[0], o_sems.at[1], partner)

    def keep(k):
        cols = pl.ds(512 * k, 512)
        return pltpu.make_async_copy(o_own.at[:, cols], out.at[:, cols], o_sems.at[2 + k])

    scores_into(1, 2 * pairs - 1)
    attend(0, 2 * pairs - 2)
    for h in range(12):
        project(h)
    attend(1, 2 * pairs - 1)
    pl.when(y < 3)(lambda: keep(0).start())
    keep(1).start()
    keep(2).start()

    @pl.when(y == 0)
    def _():
        for h in range(4):
            o_guest[:, h * VDIM : (h + 1) * VDIM] = through(mixed_of(GUEST * TQ + h * TOK), h)
        home.start()

    for h in range(12, HEADS):
        project(h)
    keep(3).start()
    for copy in sends:
        copy.wait_send()
    for w, plane_y in enumerate((below, above)):
        to_sibling(4 + 4 * w, plane_y, 1, 3).wait_send()
        to_sibling(5 + 4 * w, plane_y, 0, 1).wait_send()
        to_sibling(6 + 4 * w, plane_y, 4, 1).wait_send()
        to_sibling(7 + 4 * w, plane_y, FAR, 3).wait_send()
    to_sibling(0, y, 1, 3).wait_send()
    to_sibling(1, y, 0, 1).wait_send()
    to_sibling(2, y, 4, 1).wait_send()
    to_sibling(3, y, FAR, 3).wait_send()
    to_sibling(12, across, 0, NZ).wait_send()
    pl.when(y < 3)(lambda: keep(0).wait())
    for k in (1, 2, 3):
        keep(k).wait()

    @pl.when(y == 0)
    def _():
        home.wait_send()

    @pl.when(y == 3)
    def _():
        q_copy.wait_send()
        home.wait_recv()


def hand_over(a, b, a_out, b_out):
    a_out[...] = a[...]
    b_out[...] = b[...]


def on_device(
    prefill_hidden, down_weight, latent_gain, key_weight, value_weight, prefill_query,
    decode_hidden, decode_query, latent_cache, place_device, place_slot, context_length,
):
    half = ROPE // 2
    freq = 10000.0 ** (-(np.arange(128) % half).astype(np.float64) / half)
    freq = jnp.asarray(freq.astype(np.float32)[None])
    vmem = pl.BlockSpec(memory_space=pltpu.VMEM)
    hbm = pl.BlockSpec(memory_space=pl.ANY)
    dma = pltpu.SemaphoreType.DMA
    out, dec_out = pl.pallas_call(
        kernel,
        out_shape=(
            jax.ShapeDtypeStruct((TOK, HEADS * VDIM), bf16),
            jax.ShapeDtypeStruct((2, 4, HEADS * VDIM), bf16),
        ),
        in_specs=[hbm] * 8 + [pl.BlockSpec(memory_space=pltpu.SMEM)] + [hbm] * 4,
        out_specs=(hbm, vmem),
        scratch_shapes=[
            pltpu.VMEM((TOK, 896), bf16),
            pltpu.VMEM((LAT + ROPE, 896), bf16),
            pltpu.VMEM((2, 4, 896), bf16),
            pltpu.VMEM((1, LAT), f32),
            pltpu.VMEM((1, 128), f32),
            pltpu.VMEM((1, TOK), i32),
            pltpu.VMEM((1, TOK), i32),
            pltpu.VMEM((2, 4, HEADS * 192), bf16),
            pltpu.VMEM((LAT, HEADS * NOPE), bf16),
            pltpu.VMEM((LAT, HEADS * VDIM), bf16),
            pltpu.VMEM((TOK, HEADS * 192), bf16),
            pltpu.VMEM((TOK, 4 * 192), bf16),
            pltpu.VMEM((4, LAT + ROPE, 512), bf16),
            pltpu.VMEM((TOK, ROW), f32),
            pltpu.VMEM((8, ROW), f32),
            pltpu.VMEM((NHP - 1, 16, ROW), f32),
            pltpu.VMEM((NHP - 1, 8, ROW), f32),
            pltpu.VMEM((NY, NZ, NHP, 16, ROW), bf16),
            pltpu.VMEM((NY * NZ, 8, TOK), i32),
            pltpu.VMEM((TOK, ROW), bf16),
            pltpu.VMEM((5 * TQ, ROW), bf16),
            pltpu.VMEM((TOK, ROW), bf16),
            pltpu.VMEM((5 * TQ, 128), f32),
            pltpu.VMEM((5 * TQ, 128), f32),
            pltpu.VMEM((5 * TQ, LAT), f32),
            pltpu.VMEM((TOK, 128), f32),
            pltpu.VMEM((TOK, 128), f32),
            pltpu.VMEM((TOK, LAT), f32),
            pltpu.VMEM((TOK, 2048), f32),
            pltpu.VMEM((2, TQ, CHUNK), f32),
            pltpu.VMEM((TOK, HEADS * VDIM), bf16),
            pltpu.VMEM((TOK, 4 * VDIM), bf16),
            dma((12,)), dma((2,)), dma((7,)), dma((7,)), dma((7,)), dma((7,)),
            dma((7,)), dma((7,)), dma((3,)), dma((3,)),
            dma((3,)), dma((3,)), dma((3,)), dma((3,)), dma((4,)), dma((4,)),
            dma((12,)), dma((12,)), dma((3,)), dma((3,)), dma((4,)), dma((4,)),
            dma((3,)), dma((3,)), dma((8,)), dma((8,)), dma((13,)), dma((13,)), dma((6,)),
        ],
        compiler_params=pltpu.CompilerParams(
            collective_id=0, has_side_effects=True, vmem_limit_bytes=56 << 20
        ),
    )(
        prefill_hidden, down_weight.T, decode_hidden, latent_gain.reshape(1, LAT), freq,
        place_device.reshape(1, TOK), place_slot.reshape(1, TOK), decode_query, context_length,
        key_weight, value_weight, prefill_query, latent_cache.transpose(0, 2, 1),
    )
    return pl.pallas_call(
        hand_over,
        out_shape=(
            jax.ShapeDtypeStruct((TOK, HEADS * VDIM), bf16),
            jax.ShapeDtypeStruct((2, 4, HEADS * VDIM), bf16),
        ),
        in_specs=[vmem, vmem],
        out_specs=(vmem, vmem),
    )(out, dec_out)


def solution(mesh):
    in_specs = (
        P("seq", ("head", "pool")),
        P(("head", "pool"), None),
        P(),
        P(None, ("head", "pool")),
        P(None, ("head", "pool")),
        P("seq", ("head", "pool")),
        P(None, "seq", ("head", "pool")),
        P(None, "seq", ("head", "pool")),
        P("seq", None, None),
        P("seq"),
        P("seq"),
        P("seq"),
    )
    out_specs = (P("seq", ("head", "pool")), P(None, "seq", ("head", "pool")))
    return jax.shard_map(
        on_device, mesh=mesh, in_specs=in_specs, out_specs=out_specs, check_vma=False
    )
```

```python
import functools

import jax
import jax.numpy as jnp
import numpy as np
from jax import lax
from jax.experimental import pallas as pl
from jax.experimental.pallas import tpu as pltpu
from jax.sharding import PartitionSpec as P

LAT = 512
ROPE = 64
NOPE = 128
VDIM = 128
ROW = 640
TOK = 128
HEADS = 16
NY, NZ = 4, 8
CHUNK = NZ * TOK
NHP = 8
OWN, FAR = 2, 5
TQ = 512
GUEST = 4
SCALE = (NOPE + ROPE) ** (-0.5) * 1.4426950408889634
NEG = -1e30
MESH = pl.DeviceIdType.MESH
f32, bf16, i32 = jnp.float32, jnp.bfloat16, jnp.int32
NT = (((1,), (1,)), ((), ()))

STEPS = [
    [(0, 0), (1, 0), (2, 0), (3, 0), (0, 0), (0, 1), (0, 3), (0, 2)],
    [(t, c) for c in (1, 0) for t in range(4)],
    [(t, c) for c in (2, 1, 0) for t in range(4)],
    [(t, c) for c in (3, 2, 0, 1) for t in (1, 2, 3)],
]
TILE_CODE = [sum(t << (2 * n) for n, (t, c) in enumerate(row)) for row in STEPS]
CHUNK_CODE = [sum(c << (2 * n) for n, (t, c) in enumerate(row)) for row in STEPS]


def pick(y, table):
    return jnp.where(
        y == 0, table[0], jnp.where(y == 1, table[1], jnp.where(y == 2, table[2], table[3]))
    )


def finalize(summed, gain, freq, position):
    content = summed[:, :LAT]
    meansq = jnp.mean(content * content, -1, keepdims=True)
    content = content * lax.rsqrt(meansq + 1e-06) * gain
    tail = summed[:, LAT:]
    lane = lax.broadcasted_iota(i32, tail.shape, 1)
    angle = position * freq
    cosine, sine = jnp.cos(angle), jnp.sin(angle)
    swapped = jnp.where(lane < 32, -pltpu.roll(tail, 96, 1), pltpu.roll(tail, 32, 1))
    rotated = jnp.where(lane < ROPE, tail * cosine + swapped * sine, 0.0)
    return jnp.concatenate([content, rotated], -1).astype(bf16)


def kernel(
    hidden_in, down_in, dec_hidden_in, gain_in, freq_in, dev_in, slot_in, dec_query_in, context,
    key_w, value_w, query, cache,
    out, dec_out,
    hidden, down, dec_hidden, gain, freq, place_dev, place_slot, dec_query,
    kw, vw, q_own, q_far, kept,
    part, part_d, rs, rs_d, lat, meta, fresh,
    qa, qd, m_ref, l_ref, acc, dm, dl, dacc, ks, sbuf, o_own, o_guest,
    ld_sem, q_sems, rs_s, rs_r, rd_s, rd_r, mz_s, mz_r, my_s, my_r,
    ax_s, ax_r, fz_s, fz_r, nz_s, nz_r, xf_s, xf_r, yf_s, yf_r, yn_s, yn_r, yo_s, yo_r, zs_s, zs_r,
    sb_s, sb_r, o_sems,
):
    seq = lax.axis_index("seq")
    head = lax.axis_index("head")
    pool = lax.axis_index("pool")
    y, z = seq // NZ, seq % NZ
    hp = head * 4 + pool

    def at_hp(d):
        other = (hp + d) % NHP
        return other, {"head": other // 4, "pool": other % 4}

    def at_z(d):
        return {"seq": y * NZ + (z + d + NZ) % NZ}

    def at_y(d):
        return {"seq": (y + d + NY) % NY * NZ + z}

    def at_x(d):
        return {"pool": (pool + d) % 4}

    partner = {"seq": (NY - 1 - y) * NZ + z}
    sibling = {"head": 1 - head}

    def remote(src, dst, ssem, rsem, dev):
        return pltpu.make_async_remote_copy(
            src_ref=src, dst_ref=dst, send_sem=ssem, recv_sem=rsem, device_id=dev,
            device_id_type=MESH,
        )

    first_loads = [
        pltpu.make_async_copy(src, dst, ld_sem.at[4 + i])
        for i, (src, dst) in enumerate(
            (
                (hidden_in, hidden), (down_in, down), (dec_hidden_in, dec_hidden),
                (dev_in, place_dev), (slot_in, place_slot), (gain_in, gain), (freq_in, freq),
                (dec_query_in, dec_query),
            )
        )
    ]
    loads = [
        pltpu.make_async_copy(query, q_own, ld_sem.at[0]),
        pltpu.make_async_copy(key_w, kw, ld_sem.at[1]),
        pltpu.make_async_copy(cache, kept, ld_sem.at[2]),
        pltpu.make_async_copy(value_w, vw, ld_sem.at[3]),
    ]
    for copy in first_loads + loads:
        copy.start()

    barrier = pltpu.get_barrier_semaphore()
    for d in range(1, NHP):
        pl.semaphore_signal(barrier, inc=1, device_id=at_hp(d)[1], device_id_type=MESH)
    for d in range(1, NZ):
        pl.semaphore_signal(barrier, inc=1, device_id=at_z(d), device_id_type=MESH)
    for d in range(1, NY):
        pl.semaphore_signal(barrier, inc=1, device_id=at_y(d), device_id_type=MESH)

    for copy in first_loads:
        copy.wait()
    part[:, LAT:] = jnp.zeros((TOK, ROW - LAT), f32)
    part_d[:, LAT:] = jnp.zeros((8, ROW - LAT), f32)
    part[:, : LAT + ROPE] = lax.dot_general(
        hidden[...], down[...], NT, preferred_element_type=f32
    )
    dh = jnp.concatenate([dec_hidden[0].astype(f32), dec_hidden[1].astype(f32)], 0).astype(bf16)
    part_d[:, : LAT + ROPE] = lax.dot_general(dh, down[...], NT, preferred_element_type=f32)
    mine = meta.at[pl.ds(seq, 1)]
    meta[pl.ds(seq, 1), 0:1, :] = place_dev[...].reshape(1, 1, TOK)
    meta[pl.ds(seq, 1), 1:2, :] = place_slot[...].reshape(1, 1, TOK)

    pl.semaphore_wait(barrier, NHP + NZ + NY - 3)

    sends = []

    def go(copy):
        copy.start()
        sends.append(copy)
        return copy

    rs_copies, rd_copies = [], []
    for d in range(1, NHP):
        other, dev = at_hp(d)
        rows = pl.ds(pl.multiple_of(other * 16, 16), 16)
        rs_copies.append(
            go(remote(part.at[rows], rs.at[d - 1], rs_s.at[d - 1], rs_r.at[d - 1], dev))
        )
    mz = [
        go(remote(mine, mine, mz_s.at[d - 1], mz_r.at[d - 1], at_z(d))) for d in range(1, NZ)
    ]
    q_copy = remote(
        query.at[:, pl.ds(0, 768)], q_far, q_sems.at[0], q_sems.at[1], partner
    )
    pl.when(y == 3)(lambda: q_copy.start())

    m_ref[...] = jnp.full(m_ref.shape, NEG, f32)
    l_ref[...] = jnp.zeros(l_ref.shape, f32)
    dm[...] = jnp.full(dm.shape, NEG, f32)
    dl[...] = jnp.zeros(dl.shape, f32)
    dacc[...] = jnp.zeros(dacc.shape, f32)

    def clear(i, carry):
        acc[pl.ds(pl.multiple_of(i * 256, 256), 256), :] = jnp.zeros((256, LAT), f32)
        return carry

    lax.fori_loop(0, 5 * TQ // 256, clear, 0)

    def absorb(load, dst, base, rows, heads=HEADS):
        def pair(j, carry):
            col = pl.multiple_of(j * 384, 128)
            t0, t1, t2 = load(col), load(col + 128), load(col + 256)
            lane = lax.broadcasted_iota(i32, t0.shape, 1)
            low = lane < 64
            nopes = (t0, pltpu.roll(jnp.where(low, t2, t1), 64, 1))
            ropes = (jnp.where(low, t1, 0.0), jnp.where(low, pltpu.roll(t2, 64, 1), 0.0))
            both = []
            for k in range(2):
                wcol = pl.multiple_of(j * 256 + k * 128, 128)
                absorbed = lax.dot_general(
                    nopes[k].astype(bf16), kw[:, pl.ds(wcol, 128)], NT, preferred_element_type=f32
                )
                both.append(jnp.concatenate([absorbed, ropes[k]], -1))
            at = pl.multiple_of(base + 2 * j * rows, 2 * rows)
            dst[pl.ds(at, 2 * rows), :] = jnp.concatenate(both, 0).astype(bf16)
            return carry

        lax.fori_loop(0, heads // 2, pair, 0)

    loads[0].wait()
    loads[1].wait()
    absorb(lambda c: q_own[:, pl.ds(c, 128)].astype(f32), qa, 0, TOK)
    absorb(
        lambda c: jnp.concatenate(
            [dec_query[0, :, pl.ds(c, 128)], dec_query[1, :, pl.ds(c, 128)]], 0
        ).astype(f32),
        qd, 0, 8,
    )

    loads[2].wait()
    for r in range(4):
        ks[:, 512 * r : 512 * (r + 1)] = jnp.dot(
            qd[:, :LAT], kept[r, :LAT], preferred_element_type=f32
        ) + jnp.dot(qd[:, LAT : LAT + ROPE], kept[r, LAT:], preferred_element_type=f32)

    for copy in rs_copies:
        copy.wait_recv()
    first = seq * TOK + hp * 16
    summed = part[pl.ds(pl.multiple_of(hp * 16, 16), 16), :]
    for d in range(1, NHP):
        summed = summed + rs[d - 1]
    position = (first + lax.broadcasted_iota(i32, (16, 1), 0)).astype(f32)
    lat[y, OWN, hp] = finalize(summed, gain[...], freq[...], position)

    half = pl.ds(head * 4, 4)
    own_rows = lat.at[y, OWN, hp]
    ax = [
        go(remote(own_rows, own_rows, ax_s.at[d - 1], ax_r.at[d - 1], at_x(d))) for d in (1, 2, 3)
    ]
    fz = []
    for k, d in enumerate((3, 4, 5)):
        there = lat.at[y, (OWN - d) % NZ, hp]
        fz.append(go(remote(own_rows, there, fz_s.at[k], fz_r.at[k], at_z(d))))
    for d in range(1, NHP):
        rd_copies.append(
            go(remote(part_d, rs_d.at[d - 1], rd_s.at[d - 1], rd_r.at[d - 1], at_hp(d)[1]))
        )

    for copy in ax:
        copy.wait_recv()
    own_half = lat.at[y, OWN, half]
    nz = {}
    for k, d in enumerate((1, -1, 2, -2)):
        there = lat.at[y, OWN - d, half]
        nz[d] = go(remote(own_half, there, nz_s.at[k], nz_r.at[k], at_z(d)))

    yo = {}
    for k, d in enumerate((1, -1, 2)):
        yo[d] = go(remote(own_half, own_half, yo_s.at[k], yo_r.at[k], at_y(d)))

    below, above, across = (y + 3) % NY, (y + 1) % NY, (y + 2) % NY

    def along_z(k, plane_y, d):
        there = lat.at[plane_y, OWN - d, half]
        return go(
            remote(lat.at[plane_y, OWN, half], there, zs_s.at[k], zs_r.at[k], at_z(d))
        )

    yn = {1: [], -1: []}

    def to_planes(i):
        ref = lat.at[y, i, half]
        for w, d in enumerate((1, -1)):
            k = 2 * w + i // 4
            yn[d].append(go(remote(ref, ref, yn_s.at[k], yn_r.at[k], at_y(d))))

    for copy in mz:
        copy.wait_recv()
    plane = meta.at[pl.ds(pl.multiple_of(y * NZ, NZ), NZ)]
    my = [go(remote(plane, plane, my_s.at[d - 1], my_r.at[d - 1], at_y(d))) for d in range(1, NY)]

    def over_x(dist, plane_y):
        ref = lat.at[plane_y, pl.ds(FAR, 3), hp]
        return [
            go(
                remote(
                    ref, ref, xf_s.at[3 * dist + d - 1], xf_r.at[3 * dist + d - 1], at_x(d)
                )
            )
            for d in (1, 2, 3)
        ]

    for copy in fz:
        copy.wait_recv()
    xf = {0: over_x(0, y)}
    far_rows = lat.at[y, pl.ds(FAR, 3), hp]
    yf = [go(remote(far_rows, far_rows, yf_s.at[d - 1], yf_r.at[d - 1], at_y(d))) for d in (1, 2, 3)]

    def to_sibling(k, plane_y, start, count):
        ref = lat.at[plane_y, pl.ds(start, count), half]
        return remote(ref, ref, sb_s.at[k], sb_r.at[k], sibling)

    def from_sibling(k, plane_y, start, count):
        to_sibling(k, plane_y, start, count).wait_recv()

    ctx = [context[r] for r in range(4)]
    drow = lax.broadcasted_iota(i32, (TOK, 1), 0) % 4
    dstep = lax.broadcasted_iota(i32, (TOK, 1), 0) // 4 % 2

    def decode_weights(scores, mask):
        scores = jnp.where(mask, scores * SCALE, NEG)
        m_old = dm[...]
        m_new = jnp.maximum(m_old, jnp.max(scores, -1, keepdims=True))
        alpha = jnp.exp2(m_old - m_new)
        dm[...] = m_new
        expo = jnp.where(mask, jnp.exp2(scores - m_new[:, :1]), 0.0)
        total = dl[...] * alpha
        for j in range(scores.shape[1] // 128):
            total = total + expo[:, 128 * j : 128 * (j + 1)]
        dl[...] = total
        dacc[...] = dacc[...] * alpha[:, :1]
        return expo.astype(bf16)

    def decode_update(scores, mask, contents):
        expo = decode_weights(scores, mask)
        dacc[...] = dacc[...] + jnp.dot(expo, contents, preferred_element_type=f32)

    @pl.when(y == 0)
    def _():
        q_copy.wait_recv()
        absorb(lambda c: q_far[:, pl.ds(c, 128)].astype(f32), qa, GUEST * TQ, TOK, 4)

    yo[1].wait_recv()
    zs_below = [along_z(k, below, d) for k, d in enumerate((1, -1))]
    yo[-1].wait_recv()
    zs_above = [along_z(2 + k, above, d) for k, d in enumerate((1, -1))]
    for copy in rd_copies:
        copy.wait_recv()
    summed = part_d[...]
    for d in range(1, NHP):
        summed = summed + rs_d[d - 1]
    row8 = lax.broadcasted_iota(i32, (8, 1), 0)
    length = pick(row8 % 4, ctx)
    new_rows = finalize(summed, gain[...], freq[...], (length + row8 // 4).astype(f32))
    fresh[...] = jnp.concatenate([new_rows.astype(f32), jnp.zeros((TOK - 8, ROW), f32)], 0).astype(
        bf16
    )
    key = lax.broadcasted_iota(i32, (1, TOK), 1)
    decode_update(
        lax.dot_general(qd[...], fresh[...], NT, preferred_element_type=f32),
        (key < 8) & (key % 4 == drow) & (key // 4 <= dstep),
        fresh[:, :LAT],
    )
    for d in (1, -1):
        nz[d].wait_recv()
    to_sibling(0, y, 1, 3).start()
    yo[2].wait_recv()
    zs_across = [along_z(4 + k, across, d) for k, d in enumerate((1, -1, 2, -2))]
    for copy in my:
        copy.wait_recv()
    counts = jnp.zeros((16, TOK), f32)
    for b in range(NY * NZ):
        device, slot = meta[b, 0:1, :], meta[b, 1:2, :]
        here = device == seq
        high = jnp.where(here, slot // 128, -1)
        low = slot % 128
        one = lax.broadcasted_iota(i32, (16, TOK), 0) == high
        two = lax.broadcasted_iota(i32, (TOK, TOK), 0) == low
        counts = counts + lax.dot_general(
            one.astype(f32).astype(bf16), two.astype(f32).astype(bf16), NT,
            preferred_element_type=f32,
        )
    hi = lax.broadcasted_iota(i32, (16, TOK), 0)
    place = hi % 4 * 128 + lax.broadcasted_iota(i32, (16, TOK), 1)
    live = (place < pick(hi // 4, ctx)) & (counts < 0.5)
    owner = jnp.where(live, hi // 4, -1)

    def kept_rows():
        keyrow = jnp.concatenate([owner[j : j + 1, :] for j in range(16)], 1)
        expo = decode_weights(ks[...], keyrow == drow)
        mixed = dacc[...]
        for r in range(4):
            mixed = mixed + lax.dot_general(
                expo[:, 512 * r : 512 * (r + 1)], kept[r, :LAT], NT, preferred_element_type=f32
            )
        dacc[...] = mixed

    for d in (2, -2):
        nz[d].wait_recv()
        to_planes(OWN - d)
    to_sibling(1, y, 0, 1).start()
    to_sibling(2, y, 4, 1).start()
    for copy in xf[0]:
        copy.wait_recv()
    to_sibling(3, y, FAR, 3).start()
    for d in (1, 3, 2):
        yf[d - 1].wait_recv()
        xf[d] = over_x(d, (y - d + NY) % NY)

    kept_rows()

    def decode_chunks(*planes):
        pieces, scores = [], []
        for c in planes:
            for j in range(NZ):
                tile = meta[pl.ds(c * NZ + (z + j + 6) % NZ, 1), :, :][0]
                pieces.append(jnp.where(tile[0:1] == seq, tile[1:2] // 512, -1))
            scores.append(
                lax.dot_general(
                    qd[...], lat[c].reshape(CHUNK, ROW), NT, preferred_element_type=f32
                )
            )
        expo = decode_weights(jnp.concatenate(scores, 1), jnp.concatenate(pieces, 1) == drow)
        mixed = dacc[...]
        for k, c in enumerate(planes):
            mixed = mixed + jnp.dot(
                expo[:, CHUNK * k : CHUNK * (k + 1)], lat[c, :, :, :, :LAT].reshape(CHUNK, LAT),
                preferred_element_type=f32,
            )
        dacc[...] = mixed

    tile_code, chunk_code = pick(y, TILE_CODE), pick(y, CHUNK_CODE)

    def step_of(n):
        tile = jnp.where((y == 0) & (n >= 4), GUEST, (tile_code >> (2 * n)) & 3)
        return tile, (chunk_code >> (2 * n)) & 3

    def rows_of(tile):
        return pl.ds(pl.multiple_of(tile * TQ, TQ), TQ)

    def scores_into(slot, n):
        tile, c = step_of(n)
        sbuf[slot] = lax.dot_general(
            qa[rows_of(tile), :], lat[c].reshape(CHUNK, ROW), NT, preferred_element_type=f32
        )

    def attend(slot, n):
        tile, c = step_of(n)
        rows = rows_of(tile)
        limit = jnp.where(tile == GUEST, 3, y)
        start = jnp.where(c == limit, z * TOK, 1 << 20)
        token = start + lax.broadcasted_iota(i32, (TQ, 1), 0) % TOK
        key = (lax.broadcasted_iota(i32, (1, CHUNK), 1) + (z + 6) * TOK) & (CHUNK - 1)
        allowed = key <= token
        scores = jnp.where(allowed, sbuf[slot], NEG)
        m_old = m_ref[rows, :]
        m_new = jnp.maximum(m_old, jnp.max(scores, -1, keepdims=True) * SCALE)
        alpha = jnp.exp2(m_old - m_new)
        m_ref[rows, :] = m_new
        expo = jnp.exp2(scores * SCALE - m_new[:, :1])
        total = l_ref[rows, :] * alpha
        for j in range(CHUNK // 128):
            total = total + expo[:, 128 * j : 128 * (j + 1)]
        l_ref[rows, :] = total
        acc[rows, :] = acc[rows, :] * alpha[:, :1] + jnp.dot(
            expo.astype(bf16), lat[c, :, :, :, :LAT].reshape(CHUNK, LAT), preferred_element_type=f32
        )

    def near_arrive():
        for w, (plane_y, spread) in enumerate(((below, zs_below), (above, zs_above))):
            for copy in spread:
                copy.wait_recv()
            to_sibling(4 + 4 * w, plane_y, 1, 3).start()
        for w, (d, dist, plane_y) in enumerate(((1, 1, below), (-1, 3, above))):
            for k, copy in enumerate(yn[d]):
                copy.wait_recv()
                to_sibling(5 + 4 * w + k, plane_y, (0, 4)[k], 1).start()
            for copy in xf[dist]:
                copy.wait_recv()
            to_sibling(7 + 4 * w, plane_y, FAR, 3).start()

    def near_there(w):
        plane_y = (below, above)[w]
        from_sibling(4 + 4 * w, plane_y, 1, 3)
        from_sibling(5 + 4 * w, plane_y, 0, 1)
        from_sibling(6 + 4 * w, plane_y, 4, 1)
        from_sibling(7 + 4 * w, plane_y, FAR, 3)

    def far_arrive():
        for copy in zs_across + xf[2]:
            copy.wait_recv()
        to_sibling(12, across, 0, NZ).start()

    from_sibling(0, y, 1, 3)
    from_sibling(1, y, 0, 1)
    from_sibling(2, y, 4, 1)
    from_sibling(3, y, FAR, 3)
    scores_into(0, 0)
    upper = y >= 2

    def near_first():
        near_arrive()
        near_there(0)

    def two_steps(i, carry):
        pl.when((i == 1) & (y == 3))(near_first)
        scores_into(1, 2 * i + 1)
        attend(0, 2 * i)
        pl.when((i == 1) & (y < 3))(near_first)
        pl.when(i == jnp.where(upper, 2, 1))(lambda: near_there(1))
        pl.when(i == 2)(far_arrive)
        pl.when(i == jnp.where(upper, 3, 2))(lambda: from_sibling(12, across, 0, NZ))
        scores_into(0, 2 * i + 2)
        attend(1, 2 * i + 1)
        return carry

    pairs = jnp.where(upper, 6, 4)
    lax.fori_loop(0, pairs - 1, two_steps, 0)

    loads[3].wait()
    scores_into(1, 2 * pairs - 1)
    attend(0, 2 * pairs - 2)
    decode_chunks(y, below, above, across)

    dmixed = dacc[...] * (1.0 / jnp.sum(dl[...], -1, keepdims=True))

    def mixed_of(row):
        rows = pl.ds(row, TOK)
        return acc[rows, :] * (1.0 / jnp.sum(l_ref[rows, :], -1, keepdims=True))

    def through(mixed, h):
        weight = vw[:, h * VDIM : (h + 1) * VDIM]
        return jnp.dot(mixed.astype(bf16), weight, preferred_element_type=f32).astype(bf16)

    def project(h):
        both = jnp.concatenate([mixed_of(h * TOK), dmixed[8 * h : 8 * h + 8]], 0)
        res = through(both, h)
        col = slice(h * VDIM, (h + 1) * VDIM)
        o_own[:, col] = res[:TOK]
        dec_out[0, :, col] = res[TOK : TOK + 4]
        dec_out[1, :, col] = res[TOK + 4 :]

    home = remote(o_guest, out.at[:, pl.ds(0, 512)], o_sems.at[0], o_sems.at[1], partner)

    def keep(k):
        cols = pl.ds(512 * k, 512)
        return pltpu.make_async_copy(o_own.at[:, cols], out.at[:, cols], o_sems.at[2 + k])

    for h in range(12):
        project(h)
    attend(1, 2 * pairs - 1)
    pl.when(y < 3)(lambda: keep(0).start())
    keep(1).start()
    keep(2).start()

    @pl.when(y == 0)
    def _():
        for h in range(4):
            o_guest[:, h * VDIM : (h + 1) * VDIM] = through(mixed_of(GUEST * TQ + h * TOK), h)
        home.start()

    for h in range(12, HEADS):
        project(h)
    keep(3).start()
    for copy in sends:
        copy.wait_send()
    for w, plane_y in enumerate((below, above)):
        to_sibling(4 + 4 * w, plane_y, 1, 3).wait_send()
        to_sibling(5 + 4 * w, plane_y, 0, 1).wait_send()
        to_sibling(6 + 4 * w, plane_y, 4, 1).wait_send()
        to_sibling(7 + 4 * w, plane_y, FAR, 3).wait_send()
    to_sibling(0, y, 1, 3).wait_send()
    to_sibling(1, y, 0, 1).wait_send()
    to_sibling(2, y, 4, 1).wait_send()
    to_sibling(3, y, FAR, 3).wait_send()
    to_sibling(12, across, 0, NZ).wait_send()
    pl.when(y < 3)(lambda: keep(0).wait())
    for k in (1, 2, 3):
        keep(k).wait()

    @pl.when(y == 0)
    def _():
        home.wait_send()

    @pl.when(y == 3)
    def _():
        q_copy.wait_send()
        home.wait_recv()


def hand_over(a, b, a_out, b_out):
    a_out[...] = a[...]
    b_out[...] = b[...]


def on_device(
    prefill_hidden, down_weight, latent_gain, key_weight, value_weight, prefill_query,
    decode_hidden, decode_query, latent_cache, place_device, place_slot, context_length,
):
    half = ROPE // 2
    freq = 10000.0 ** (-(np.arange(128) % half).astype(np.float64) / half)
    freq = jnp.asarray(freq.astype(np.float32)[None])
    vmem = pl.BlockSpec(memory_space=pltpu.VMEM)
    hbm = pl.BlockSpec(memory_space=pl.ANY)
    dma = pltpu.SemaphoreType.DMA
    out, dec_out = pl.pallas_call(
        kernel,
        out_shape=(
            jax.ShapeDtypeStruct((TOK, HEADS * VDIM), bf16),
            jax.ShapeDtypeStruct((2, 4, HEADS * VDIM), bf16),
        ),
        in_specs=[hbm] * 8 + [pl.BlockSpec(memory_space=pltpu.SMEM)] + [hbm] * 4,
        out_specs=(hbm, vmem),
        scratch_shapes=[
            pltpu.VMEM((TOK, 896), bf16),
            pltpu.VMEM((LAT + ROPE, 896), bf16),
            pltpu.VMEM((2, 4, 896), bf16),
            pltpu.VMEM((1, LAT), f32),
            pltpu.VMEM((1, 128), f32),
            pltpu.VMEM((1, TOK), i32),
            pltpu.VMEM((1, TOK), i32),
            pltpu.VMEM((2, 4, HEADS * 192), bf16),
            pltpu.VMEM((LAT, HEADS * NOPE), bf16),
            pltpu.VMEM((LAT, HEADS * VDIM), bf16),
            pltpu.VMEM((TOK, HEADS * 192), bf16),
            pltpu.VMEM((TOK, 4 * 192), bf16),
            pltpu.VMEM((4, LAT + ROPE, 512), bf16),
            pltpu.VMEM((TOK, ROW), f32),
            pltpu.VMEM((8, ROW), f32),
            pltpu.VMEM((NHP - 1, 16, ROW), f32),
            pltpu.VMEM((NHP - 1, 8, ROW), f32),
            pltpu.VMEM((NY, NZ, NHP, 16, ROW), bf16),
            pltpu.VMEM((NY * NZ, 8, TOK), i32),
            pltpu.VMEM((TOK, ROW), bf16),
            pltpu.VMEM((5 * TQ, ROW), bf16),
            pltpu.VMEM((TOK, ROW), bf16),
            pltpu.VMEM((5 * TQ, 128), f32),
            pltpu.VMEM((5 * TQ, 128), f32),
            pltpu.VMEM((5 * TQ, LAT), f32),
            pltpu.VMEM((TOK, 128), f32),
            pltpu.VMEM((TOK, 128), f32),
            pltpu.VMEM((TOK, LAT), f32),
            pltpu.VMEM((TOK, 2048), f32),
            pltpu.VMEM((2, TQ, CHUNK), f32),
            pltpu.VMEM((TOK, HEADS * VDIM), bf16),
            pltpu.VMEM((TOK, 4 * VDIM), bf16),
            dma((12,)), dma((2,)), dma((7,)), dma((7,)), dma((7,)), dma((7,)),
            dma((7,)), dma((7,)), dma((3,)), dma((3,)),
            dma((3,)), dma((3,)), dma((3,)), dma((3,)), dma((4,)), dma((4,)),
            dma((12,)), dma((12,)), dma((3,)), dma((3,)), dma((4,)), dma((4,)),
            dma((3,)), dma((3,)), dma((8,)), dma((8,)), dma((13,)), dma((13,)), dma((6,)),
        ],
        compiler_params=pltpu.CompilerParams(
            collective_id=0, has_side_effects=True, vmem_limit_bytes=56 << 20
        ),
    )(
        prefill_hidden, down_weight.T, decode_hidden, latent_gain.reshape(1, LAT), freq,
        place_device.reshape(1, TOK), place_slot.reshape(1, TOK), decode_query, context_length,
        key_weight, value_weight, prefill_query, latent_cache.transpose(0, 2, 1),
    )
    return pl.pallas_call(
        hand_over,
        out_shape=(
            jax.ShapeDtypeStruct((TOK, HEADS * VDIM), bf16),
            jax.ShapeDtypeStruct((2, 4, HEADS * VDIM), bf16),
        ),
        in_specs=[vmem, vmem],
        out_specs=(vmem, vmem),
    )(out, dec_out)


def solution(mesh):
    in_specs = (
        P("seq", ("head", "pool")),
        P(("head", "pool"), None),
        P(),
        P(None, ("head", "pool")),
        P(None, ("head", "pool")),
        P("seq", ("head", "pool")),
        P(None, "seq", ("head", "pool")),
        P(None, "seq", ("head", "pool")),
        P("seq", None, None),
        P("seq"),
        P("seq"),
        P("seq"),
    )
    out_specs = (P("seq", ("head", "pool")), P(None, "seq", ("head", "pool")))
    return jax.shard_map(
        on_device, mesh=mesh, in_specs=in_specs, out_specs=out_specs, check_vma=False
    )
```
